128 devices in a mesh: ctx: 16 (over z_hi, x, core), tp: 8 (over y, z_lo).
Axes of the slice: x: 4, y: 4, z: 4 (z_hi: 2, z_lo: 2; z = z_hi * 2 + z_lo), core: 2. Of those that a mesh axis runs over, the one named last changes fastest.
Arguments:
- hidden_in: bfloat16 [4096, 4096], P('ctx', 'tp'), may hold values from -6 to 6
- upstream: bfloat16 [4096, 4096], P('ctx', 'tp'), may hold values from -6 to 6
- query_ckpt: bfloat16 [4096, 4096], P('ctx', 'tp'), may hold values from -110 to 110
- keyval_ckpt: bfloat16 [4096, 2048], P('ctx', 'tp'), may hold values from -5.5 to 5.5
- attn_out_grad: bfloat16 [4096, 4096], P('ctx', 'tp'), may hold values from -6 to 6
- segments: int32 [4096], replicated, may hold values from 0 to 1, never falling along the last dimension, each value on 1 to 3072 neighbouring positions
- query_weight: bfloat16 [4096, 4096], P(None, 'tp'), may hold values from -0.09375 to 0.09375
- keyval_weight: bfloat16 [4096, 2048], P(None, 'tp'), may hold values from -0.125 to 0.125
- mix_weight: bfloat16 [4096, 8192], P(None, 'tp'), may hold values from -0.0625 to 0.0625
- out_weight: bfloat16 [8192, 4096], P('tp'), may hold values from -0.09375 to 0.09375
- state_in_ckpt: bfloat16 [4096, 1024], P('ctx', 'tp'), may hold values from -3 to 3
- state_out_ckpt: bfloat16 [4096, 1024], P('ctx', 'tp'), may hold values from -3 to 3
- step_size: float32 [4096, 128], P('ctx', 'tp'), may hold values from 0.004 to 0.04
- decay_rate: float32 [128], P('tp'), may hold values from 0.02 to 20
- skip_gain: float32 [128], P('tp'), may hold values from 0.5 to 1.5
Outputs:
- grad_mid: bfloat16 [4096, 4096], P('ctx', 'tp')
- grad_hidden: bfloat16 [4096, 4096], P('ctx', 'tp')
- grad_state_in: float32 [4096, 1024], P('ctx', 'tp')
The draws below stay inside these ranges and needn't reach their ends.
Inputs may be any that keep to these rules, and one draw needn't show every extreme that they name: `segments`: document ids never fall along the sequence; every document has 1 to 3072 tokens.
All inputs are finite; a program needn't handle non-finite values.
Results may differ from the reference program's by a relative error of at most 0.02.
Values may be sent and summed in bfloat16 or wider, within the bound.
A program may use at most 192 MiB of HBM per device.

```python
import math
from functools import partial
import jax
import jax.numpy as jnp
import numpy as np
from jax import lax

D = 4096
HEAD = 128
QH_DEV = 4
MH_DEV = 16
PM = 64
STATE = 128
TOK_DEV = 256
TOKENS = 4096
N_TP = 8


def shared_keyval(key):
    base_rows = jax.random.normal(key, (TOKENS, N_TP * 2 * HEAD), jnp.float32)
    return jnp.clip(base_rows, -5.5, 5.5)


def draw_keyval_ckpt(key, part):
    base_rows = shared_keyval(key)
    return base_rows.astype(jnp.bfloat16)


def draw_query_ckpt(key, part):
    key = jax.random.fold_in(key, 11)
    split_one = jax.random.fold_in(key, 0)
    query_rows = jnp.clip(jax.random.normal(split_one, (TOKENS, QH_DEV * N_TP * HEAD), jnp.float32), -5.5, 5.5)
    return query_rows.astype(jnp.bfloat16)


def level_of(stream_key, shape, cuts, least, high):
    factor_of = 1.0
    for axis_at, shards_of in cuts:
        heights = jax.random.uniform(jax.random.fold_in(jax.random.fold_in(stream_key, 6), axis_at), (shards_of,), jnp.float32, least / len(cuts), high / len(cuts))
        factor_of = factor_of * jnp.repeat(jnp.exp(heights), shape[axis_at] // shards_of).reshape((-1,) + (1,) * (len(shape) - 1 - axis_at))
    return factor_of


def length_profile(number_of, total, reach, slope):
    portions = [(1 << 20) // math.isqrt(grade ** slope) + 1 for grade in range(2, number_of + 1)]
    rest, holding = total - reach - (number_of - 1), [1] * (number_of - 1)
    while rest > 0:
        candidates = [i for i in range(number_of - 1) if holding[i] < reach]
        mass, remaining = sum([portions[i] for i in candidates]), rest
        for i in candidates:
            addition = min(reach - holding[i], max(1, remaining * portions[i] // mass), rest)
            holding[i] = holding[i] + addition
            rest = rest - addition
    return np.array([reach] + holding)


def uneven(own_key, count, total, most, lean):
    if count == 2:
        one = jax.random.randint(own_key, (), max(1, total - most), min(most, total - 1) + 1)
        return jnp.stack([one, total - one])
    tallies = jnp.asarray(length_profile(count, total, most, lean), jnp.int32)
    pairs = (count - 1) // 2
    giver, taker = tallies[1:1 + 2 * pairs:2], tallies[2:2 + 2 * pairs:2]
    margin = jnp.minimum(giver - 1, most - taker)
    shifted = jax.random.randint(jax.random.fold_in(own_key, 1), (pairs,), 0, 1 << 20) % (margin + 1)
    tallies = tallies.at[1:1 + 2 * pairs:2].set(giver - shifted).at[2:2 + 2 * pairs:2].set(taker + shifted)
    return tallies[jax.random.permutation(jax.random.fold_in(own_key, 2), count)]


def gaussian(stream_key, shape, deviation, bound, cuts=(), held_as=jnp.bfloat16):
    values = deviation * jax.random.normal(stream_key, shape, jnp.float32)
    if cuts:
        values = values * level_of(stream_key, shape, cuts, -0.22, 0.18)
    return jnp.clip(values, -bound, bound).astype(held_as)


def setup_inputs(seed: int = 0) -> dict:
    splits = jax.random.split(jax.random.key(seed), 16)
    hidden_in = gaussian(splits[0], (TOKENS, D), 1.0, 6.0, ((0, 16), (1, 8)))
    upstream = gaussian(splits[1], (TOKENS, D), 1.0, 6.0, ((0, 16), (1, 8)))
    query_ckpt = draw_query_ckpt(jax.random.fold_in(splits[15], 71), 0)
    keyval_ckpt = draw_keyval_ckpt(jax.random.fold_in(splits[15], 71), 0)
    attn_out_grad = gaussian(splits[4], (TOKENS, QH_DEV * N_TP * HEAD), 1.0, 6.0, ((0, 16), (1, 8)))
    segments = jnp.searchsorted(jnp.cumsum(uneven(splits[5], 2, TOKENS, 3 * TOKENS // 4, 0)), jnp.arange(TOKENS), side="right").astype(jnp.int32)
    query_weight = gaussian(splits[6], (D, QH_DEV * N_TP * HEAD), (QH_DEV * N_TP * HEAD) ** -0.5, 0.09375, ((1, 8),))
    keyval_weight = gaussian(splits[7], (D, 2 * N_TP * HEAD), (2 * N_TP * HEAD) ** -0.5, 0.125, ((1, 8),))
    mix_weight = gaussian(splits[8], (D, MH_DEV * N_TP * PM), (MH_DEV * N_TP * PM) ** -0.5, 0.0625, ((1, 8),))
    out_weight = gaussian(splits[9], (MH_DEV * N_TP * PM, D), D ** -0.5, 0.09375, ((0, 8),))
    state_in_ckpt = gaussian(splits[10], (TOKENS, N_TP * STATE), 0.5, 3.0, ((0, 16), (1, 8)))
    state_out_ckpt = gaussian(splits[11], (TOKENS, N_TP * STATE), 0.5, 3.0, ((0, 16), (1, 8)))
    step_size = jnp.clip(jnp.exp(math.log(0.04) - 2.30258502 * jax.random.uniform(splits[12], (TOKENS, MH_DEV * N_TP), jnp.float32) ** level_of(splits[12], (TOKENS, MH_DEV * N_TP), ((0, 16), (1, 8)), -0.2, 0.2)), 0.004, 0.04)
    decay_rate = jnp.clip(jnp.exp(math.log(20.0) - 6.9077553 * jax.random.uniform(splits[13], (MH_DEV * N_TP,), jnp.float32) ** level_of(splits[13], (MH_DEV * N_TP,), ((0, 8),), -0.2, 0.2)), 0.02, 20.0)
    skip_gain = jnp.clip(1.0 + 0.1 * jax.random.normal(splits[14], (MH_DEV * N_TP,), jnp.float32), 0.5, 1.5)
    return {"hidden_in": hidden_in, "upstream": upstream, "query_ckpt": query_ckpt, "keyval_ckpt": keyval_ckpt, "attn_out_grad": attn_out_grad, "segments": segments, "query_weight": query_weight, "keyval_weight": keyval_weight, "mix_weight": mix_weight, "out_weight": out_weight, "state_in_ckpt": state_in_ckpt, "state_out_ckpt": state_out_ckpt, "step_size": step_size, "decay_rate": decay_rate, "skip_gain": skip_gain}


HIGH = lax.Precision.HIGHEST


def head_backward(allowed, inputs):
    query_rows, key_rows, value_rows, grad_rows = inputs
    scaling = query_rows.shape[1] ** -0.5
    scores = jnp.dot(query_rows, key_rows.T, preferred_element_type=jnp.float32) * scaling
    scores = jnp.where(allowed, scores, -jnp.inf)
    row_max = jnp.max(scores, axis=1, keepdims=True)
    exponent = jnp.where(allowed, jnp.exp(scores - row_max), 0.0)
    softmax = exponent / jnp.sum(exponent, axis=1, keepdims=True)
    weights_b = softmax.astype(jnp.bfloat16)
    output = jnp.dot(weights_b, value_rows, preferred_element_type=jnp.float32)
    correction = jnp.sum(grad_rows.astype(jnp.float32) * output, axis=1, keepdims=True)
    prob_grad = jnp.dot(grad_rows, value_rows.T, preferred_element_type=jnp.float32)
    score_grad = (softmax * (prob_grad - correction) * scaling).astype(jnp.bfloat16)
    query_grad = jnp.dot(score_grad, key_rows, preferred_element_type=jnp.float32)
    key_grad = jnp.dot(score_grad.T, query_rows, preferred_element_type=jnp.float32)
    value_grad = jnp.dot(weights_b.T, grad_rows, preferred_element_type=jnp.float32)
    return query_grad, key_grad, value_grad


def block_backward(skip_gain, carried_in, pieces):
    mixed_rows, grad_rows, in_rows, out_rows, step_rows, log_step = pieces
    row_count = mixed_rows.shape[0]
    cumulative = jnp.cumsum(log_step, axis=0)
    later_mask = (jnp.arange(row_count)[None, :] >= jnp.arange(row_count)[:, None])[None]
    spread = cumulative.T[:, None, :] - cumulative.T[:, :, None]
    decay_mat = jnp.where(later_mask, jnp.exp(jnp.where(later_mask, spread, 0.0)), 0.0)
    grad_float = grad_rows.astype(jnp.float32)
    mixed_float = mixed_rows.astype(jnp.float32)
    in_float = in_rows.astype(jnp.float32)
    out_float = out_rows.astype(jnp.float32)
    inner_bc = jnp.einsum('shn,thn->hst', in_float, out_float, precision=HIGH)
    local_part = jnp.einsum('hst,thp->shp', inner_bc * decay_mat, grad_float, precision=HIGH)
    to_end = jnp.exp(cumulative[-1][None, :] - cumulative)[:, :, None]
    carried = jnp.einsum('shn,hpn->shp', in_float, carried_in, precision=HIGH) * to_end
    mixed_grad = (step_rows[:, :, None] * (local_part + carried) + skip_gain[None, :, None] * grad_float).astype(jnp.bfloat16)
    pair_mat = jnp.einsum('shp,thp->hst', mixed_float, grad_float, precision=HIGH) * decay_mat
    state_local = jnp.einsum('hst,thn->shn', pair_mat, out_float, precision=HIGH)
    state_carried = jnp.einsum('shp,hpn->shn', mixed_float, carried_in, precision=HIGH) * to_end
    state_grad = step_rows[:, :, None] * (state_local + state_carried)
    contribution = jnp.einsum('thp,thn->hpn', grad_float * jnp.exp(cumulative)[:, :, None], out_float, precision=HIGH)
    new_carry = contribution + jnp.exp(cumulative[-1])[:, None, None] * carried_in
    return new_carry, (mixed_grad, state_grad)


def reference(hidden_in, upstream, query_ckpt, keyval_ckpt, attn_out_grad, segments, query_weight, keyval_weight, mix_weight, out_weight, state_in_ckpt, state_out_ckpt, step_size, decay_rate, skip_gain):
    total_rows = hidden_in.shape[0]
    query_count = QH_DEV * N_TP
    positions = jnp.arange(total_rows)
    allowed = (positions[None, :] <= positions[:, None]) & (segments[None, :] == segments[:, None])
    query_heads = query_ckpt.reshape(total_rows, query_count, HEAD).transpose(1, 0, 2)
    grad_heads = attn_out_grad.reshape(total_rows, query_count, HEAD).transpose(1, 0, 2)
    keyval_four = keyval_ckpt.reshape(total_rows, N_TP, 2, HEAD)
    key_heads = jnp.repeat(keyval_four[:, :, 0, :], QH_DEV, axis=1).transpose(1, 0, 2)
    value_heads = jnp.repeat(keyval_four[:, :, 1, :], QH_DEV, axis=1).transpose(1, 0, 2)
    query_grad, key_grad, value_grad = lax.map(partial(head_backward, allowed), (query_heads, key_heads, value_heads, grad_heads))
    query_grad = query_grad.transpose(1, 0, 2).reshape(total_rows, query_count * HEAD).astype(jnp.bfloat16)
    key_sum = key_grad.reshape(N_TP, QH_DEV, total_rows, HEAD).sum(axis=1)
    value_sum = value_grad.reshape(N_TP, QH_DEV, total_rows, HEAD).sum(axis=1)
    keyval_grad = jnp.stack([key_sum, value_sum], axis=2).transpose(1, 0, 2, 3).reshape(total_rows, N_TP * 2 * HEAD).astype(jnp.bfloat16)
    attn_partial = jnp.dot(query_grad, query_weight.T, preferred_element_type=jnp.float32) + jnp.dot(keyval_grad, keyval_weight.T, preferred_element_type=jnp.float32)
    grad_mid = (upstream.astype(jnp.float32) + attn_partial).astype(jnp.bfloat16)

    mixed = jnp.dot(hidden_in, mix_weight, preferred_element_type=jnp.float32).astype(jnp.bfloat16)
    mix_out_grad = jnp.dot(grad_mid, out_weight.T, preferred_element_type=jnp.float32).astype(jnp.bfloat16)
    mamba_count = MH_DEV * N_TP
    block_count = total_rows // TOK_DEV
    log_step = -decay_rate[None, :] * step_size
    group_of = jnp.arange(mamba_count) // MH_DEV
    in_heads = state_in_ckpt.reshape(total_rows, N_TP, STATE)[:, group_of, :]
    out_heads = state_out_ckpt.reshape(total_rows, N_TP, STATE)[:, group_of, :]

    def stacked(array):
        return array.reshape((block_count, TOK_DEV) + array.shape[1:])

    pieces = (stacked(mixed.reshape(total_rows, mamba_count, PM)), stacked(mix_out_grad.reshape(total_rows, mamba_count, PM)), stacked(in_heads), stacked(out_heads), stacked(step_size), stacked(log_step))
    start_carry = jnp.zeros((mamba_count, PM, STATE), jnp.float32)
    final_carry, (mixed_grad, state_grad) = lax.scan(partial(block_backward, skip_gain), start_carry, pieces, reverse=True)
    mixed_grad = mixed_grad.reshape(total_rows, mamba_count * PM)
    grad_state_in = state_grad.reshape(total_rows, N_TP, MH_DEV, STATE).sum(axis=2).reshape(total_rows, N_TP * STATE)
    grad_hidden = (grad_mid.astype(jnp.float32) + jnp.dot(mixed_grad, mix_weight.T, preferred_element_type=jnp.float32)).astype(jnp.bfloat16)
    return grad_mid, grad_hidden, grad_state_in
```

```python
import jax
import jax.numpy as jnp
from jax import lax
from jax.experimental import pallas as pl
from jax.experimental.pallas import tpu as pltpu
from jax.sharding import PartitionSpec as P

HIGH = lax.Precision.HIGHEST
MESH = pl.DeviceIdType.MESH
VM = pl.BlockSpec(memory_space=pltpu.VMEM)
F32 = jnp.float32
BF16 = jnp.bfloat16


def remote(src, dst, send, recv, to):
    return pltpu.make_async_remote_copy(
        src_ref=src, dst_ref=dst, send_sem=send, recv_sem=recv, device_id=to, device_id_type=MESH
    )


def greet(peers):
    barrier = pltpu.get_barrier_semaphore()
    for peer in peers:
        pl.semaphore_signal(barrier, inc=1, device_id=peer, device_id_type=MESH)
    pl.semaphore_wait(barrier, len(peers))


def params(cid, mib=40):
    return pltpu.CompilerParams(
        collective_id=cid, has_side_effects=True, vmem_limit_bytes=mib << 20
    )


def tp_places():
    c = lax.axis_index("ctx")
    me = lax.axis_index("tp")
    zp = me + 1 - 2 * lax.rem(me, 2)
    return c, me, zp, lax.rem(me + 2, 8), lax.rem(me + 6, 8)


def ctx_places():
    tp = lax.axis_index("tp")
    me = lax.axis_index("ctx")
    core = lax.rem(me, 2)
    x = lax.rem(me // 2, 4)
    zh = me // 8

    def at(z, place, c):
        return z * 8 + lax.rem(place, 4) * 2 + c

    return tp, me, core, x, zh, at


def gather_kernel(x_ref, out_ref, ssem, rsem, lsem):
    c, me, zp, up, down = tp_places()
    opp = lax.rem(me + 4, 8)
    half = x_ref.shape[0] // 2
    lo, hi = pl.ds(0, half), pl.ds(half, half)
    greet([(c, zp), (c, up), (c, down)])

    def cp(k, src, slot, to, part=None):
        dst = out_ref.at[slot] if part is None else out_ref.at[slot, part]
        return remote(src, dst, ssem.at[k], rsem.at[k], (c, to))

    c0 = cp(0, x_ref, me, zp)
    c1 = cp(1, x_ref, me, up)
    c2 = cp(2, x_ref, me, down)
    c0.start()
    c1.start()
    c2.start()
    mine = pltpu.make_async_copy(x_ref, out_ref.at[me], lsem)
    mine.start()
    c1.wait_recv()
    c5 = cp(5, out_ref.at[down, lo], down, up, lo)
    c5.start()
    c2.wait_recv()
    c6 = cp(6, out_ref.at[up, hi], up, down, hi)
    c6.start()
    c0.wait_recv()
    c3 = cp(3, out_ref.at[zp], zp, up)
    c4 = cp(4, out_ref.at[zp], zp, down)
    c3.start()
    c4.start()
    c5.wait_recv()
    c7 = cp(7, out_ref.at[opp, lo], opp, zp, lo)
    c7.start()
    c6.wait_recv()
    c8 = cp(8, out_ref.at[opp, hi], opp, zp, hi)
    c8.start()
    c3.wait_recv()
    c4.wait_recv()
    c7.wait_recv()
    c8.wait_recv()
    for k in (c0, c1, c2, c3, c4, c5, c6, c7, c8):
        k.wait_send()
    mine.wait()


def gather_tp(x, cid):
    rows, cols = x.shape
    return pl.pallas_call(
        gather_kernel,
        out_shape=jax.ShapeDtypeStruct((8, rows, cols), x.dtype),
        in_specs=[VM],
        out_specs=VM,
        scratch_shapes=[
            pltpu.SemaphoreType.DMA((9,)),
            pltpu.SemaphoreType.DMA((9,)),
            pltpu.SemaphoreType.DMA,
        ],
        compiler_params=params(cid),
        name="gather_tp",
    )(x)


def scatter_kernel(p_ref, add_ref, out_ref, tin, uin, win, vin, tout, uout, vout, ssem, rsem):
    c, me, zp, up, down = tp_places()
    opp = lax.rem(me + 4, 8)

    def other(k):
        return k + 1 - 2 * lax.rem(k, 2)

    half = out_ref.shape[0] // 2
    lo, hi = pl.ds(0, half), pl.ds(half, half)
    greet([(c, zp), (c, up), (c, down)])

    def cp(k, src, dst, to):
        return remote(src, dst, ssem.at[k], rsem.at[k], (c, to))

    a = cp(0, p_ref.at[other(opp)], tin, zp)
    a.start()
    w0 = cp(1, p_ref.at[other(up)], win.at[0], up)
    w1 = cp(2, p_ref.at[other(down)], win.at[1], down)
    w0.start()
    w1.start()
    a.wait_recv()
    tout[...] = (p_ref[opp].astype(F32) + tin[...].astype(F32)).astype(BF16)
    t0 = cp(3, tout.at[lo], uin.at[0], up)
    t1 = cp(4, tout.at[hi], uin.at[1], down)
    t0.start()
    t1.start()
    w0.wait_recv()
    w1.wait_recv()
    vout[...] = (p_ref[zp].astype(F32) + win[0].astype(F32) + win[1].astype(F32)).astype(BF16)
    v = cp(5, vout, vin, zp)
    v.start()
    t0.wait_recv()
    uout[0, lo] = (p_ref[up, lo].astype(F32) + uin[0].astype(F32)).astype(BF16)
    uout[0, hi] = p_ref[up, hi]
    u0 = cp(6, uout.at[0], win.at[2], up)
    u0.start()
    t1.wait_recv()
    uout[1, hi] = (p_ref[down, hi].astype(F32) + uin[1].astype(F32)).astype(BF16)
    uout[1, lo] = p_ref[down, lo]
    u1 = cp(7, uout.at[1], win.at[3], down)
    u1.start()
    v.wait_recv()
    acc = p_ref[me].astype(F32) + add_ref[...].astype(F32) + vin[...].astype(F32)
    u0.wait_recv()
    u1.wait_recv()
    out_ref[...] = (acc + win[2].astype(F32) + win[3].astype(F32)).astype(BF16)
    for k in (a, w0, w1, t0, t1, v, u0, u1):
        k.wait_send()


def scatter_tp(p, add, cid):
    full = p.shape[1:]
    return pl.pallas_call(
        scatter_kernel,
        out_shape=jax.ShapeDtypeStruct(full, BF16),
        in_specs=[VM, VM],
        out_specs=VM,
        scratch_shapes=[
            pltpu.VMEM(full, BF16),
            pltpu.VMEM((2, full[0] // 2, full[1]), BF16),
            pltpu.VMEM((4,) + full, BF16),
            pltpu.VMEM(full, BF16),
            pltpu.VMEM(full, BF16),
            pltpu.VMEM((2,) + full, BF16),
            pltpu.VMEM(full, BF16),
            pltpu.SemaphoreType.DMA((8,)),
            pltpu.SemaphoreType.DMA((8,)),
        ],
        compiler_params=params(cid),
        name="scatter_tp",
    )(p, add)


def gather_ctx_kernel(x_ref, out_ref, ssem, rsem, lsem):
    tp, me, core, x, zh, at = ctx_places()
    mate = at(zh, x, 1 - core)
    right, left = at(zh, x + 1, core), at(zh, x + 3, core)
    zp = at(1 - zh, x, core)
    half = x_ref.shape[0] // 2
    lo, hi = pl.ds(0, half), pl.ds(half, half)
    greet([(mate, tp), (right, tp), (left, tp), (zp, tp)])
    sent = []

    def cp(k, slot, to, part=None, own=False):
        dst = out_ref.at[slot] if part is None else out_ref.at[slot, part]
        copy = remote(x_ref if own else dst, dst, ssem.at[k], rsem.at[k], (to, tp))
        copy.start()
        sent.append(copy)
        return copy

    z0 = cp(0, me, zp, own=True)
    r0 = cp(1, me, right, own=True)
    l0 = cp(2, me, left, own=True)
    m = [cp(3, me, mate, own=True)]
    mine = pltpu.make_async_copy(x_ref, out_ref.at[me], lsem)
    mine.start()
    fr = []
    k = 4
    for z, direct in ((zh, (r0, l0)), (1 - zh, None)):
        if direct is None:
            z0.wait_recv()
            direct = (cp(k, zp, right), cp(k + 1, zp, left))
            m.append(cp(k + 2, zp, mate))
            k += 3
        direct[0].wait_recv()
        fr.append((z, cp(k, at(z, x + 3, core), right, lo)))
        m.append(cp(k + 1, at(z, x + 3, core), mate))
        direct[1].wait_recv()
        fr.append((z, cp(k + 2, at(z, x + 1, core), left, hi)))
        m.append(cp(k + 3, at(z, x + 1, core), mate))
        k += 4
    for part, (z, copy) in zip((lo, hi, lo, hi), fr):
        copy.wait_recv()
        m.append(cp(k, at(z, x + 2, core), mate, part))
        k += 1
    for copy in m:
        copy.wait_recv()
    for copy in sent:
        copy.wait_send()
    mine.wait()


def gather_ctx(x, cid):
    rows, cols = x.shape
    return pl.pallas_call(
        gather_ctx_kernel,
        out_shape=jax.ShapeDtypeStruct((16, rows, cols), x.dtype),
        in_specs=[VM],
        out_specs=VM,
        scratch_shapes=[
            pltpu.SemaphoreType.DMA((19,)),
            pltpu.SemaphoreType.DMA((19,)),
            pltpu.SemaphoreType.DMA,
        ],
        compiler_params=params(cid),
        name="gather_ctx",
    )(x)


def scatter_ctx_kernel(p_ref, out_ref, got, uin, vin, zin, tout, uout, zout, ssem, rsem):
    tp, me, core, x, zh, at = ctx_places()
    mate = at(zh, x, 1 - core)
    right, left = at(zh, x + 1, core), at(zh, x + 3, core)
    zp = at(1 - zh, x, core)
    half = out_ref.shape[0] // 2
    lo, hi = pl.ds(0, half), pl.ds(half, half)
    greet([(mate, tp), (right, tp), (left, tp), (zp, tp)])

    def cp(k, src, dst, to):
        copy = remote(src, dst, ssem.at[k], rsem.at[k], (to, tp))
        copy.start()
        return copy

    g = {}
    for k, d in enumerate((2, 1, 3, 0)):
        g[d] = cp(k, p_ref.at[:, lax.rem(x + d, 4), 1 - core], got.at[d], mate)

    def both(d):
        g[d].wait_recv()
        return p_ref[:, lax.rem(x + d, 4), core].astype(F32) + got[d].astype(F32)

    tout[...] = both(2).astype(BF16)
    t0 = cp(4, tout.at[:, lo], uin.at[0], right)
    t1 = cp(5, tout.at[:, hi], uin.at[1], left)
    q = both(1)
    t0.wait_recv()
    uout[0, :, lo] = (q[:, :half] + uin[0].astype(F32)).astype(BF16)
    uout[0, :, hi] = q[:, half:].astype(BF16)
    u0 = cp(6, uout.at[0], vin.at[0], right)
    q = both(3)
    t1.wait_recv()
    uout[1, :, hi] = (q[:, half:] + uin[1].astype(F32)).astype(BF16)
    uout[1, :, lo] = q[:, :half].astype(BF16)
    u1 = cp(7, uout.at[1], vin.at[1], left)
    g[0].wait_recv()
    u0.wait_recv()
    u1.wait_recv()

    def total(z):
        return (
            p_ref[z, x, core].astype(F32)
            + got[0, z].astype(F32)
            + vin[0, z].astype(F32)
            + vin[1, z].astype(F32)
        )

    zout[...] = total(1 - zh).astype(BF16)
    zc = cp(8, zout, zin, zp)
    mine = total(zh)
    zc.wait_recv()
    out_ref[...] = (mine + zin[...].astype(F32)).astype(BF16)
    for copy in (g[0], g[1], g[2], g[3], t0, t1, u0, u1, zc):
        copy.wait_send()


def scatter_ctx(p, cid):
    rows, cols = p.shape[-2:]
    two = (2, rows, cols)
    return pl.pallas_call(
        scatter_ctx_kernel,
        out_shape=jax.ShapeDtypeStruct((rows, cols), BF16),
        in_specs=[VM],
        out_specs=VM,
        scratch_shapes=[
            pltpu.VMEM((4,) + two, BF16),
            pltpu.VMEM((2, 2, rows // 2, cols), BF16),
            pltpu.VMEM((2,) + two, BF16),
            pltpu.VMEM((rows, cols), BF16),
            pltpu.VMEM(two, BF16),
            pltpu.VMEM((2,) + two, BF16),
            pltpu.VMEM((rows, cols), BF16),
            pltpu.SemaphoreType.DMA((9,)),
            pltpu.SemaphoreType.DMA((9,)),
        ],
        compiler_params=params(cid),
        name="scatter_ctx",
    )(p)


def prefix_kernel(s_ref, w_ref, out_ref, mine, theirs, gx, hout, hin, eout, ein, ssem, rsem):
    tp, me, core, x, zh, at = ctx_places()
    mate = at(zh, x, 1 - core)
    right, left = at(zh, x + 1, core), at(zh, x + 3, core)
    zp = at(1 - zh, x, core)
    heads = s_ref.shape[0]
    part = heads // 2
    first = core * part
    half = part // 2
    lo, hi = pl.ds(0, half), pl.ds(half, half)
    greet([(mate, tp), (right, tp), (left, tp), (zp, tp)])

    def cp(k, src, dst, to):
        copy = remote(src, dst, ssem.at[k], rsem.at[k], (to, tp))
        copy.start()
        return copy

    mine[...] = s_ref[...].astype(BF16)
    other = pl.ds((1 - core) * part, part)
    ours = pl.ds(first, part)
    c0 = cp(0, mine.at[other], theirs.at[other], mate)
    c1 = cp(1, mine.at[ours], theirs.at[ours], mate)

    def w(k, h):
        return w_ref[k, pl.ds(first + h, 1), :]

    c0.wait_recv()
    for h in range(part):
        gx[0, h] = (
            w(0, h) * s_ref[first + h] + w(1, h) * theirs[first + h].astype(F32)
        ).astype(BF16)
    r0 = cp(2, gx.at[0], gx.at[3], right)
    l0 = cp(3, gx.at[0], gx.at[1], left)
    r0.wait_recv()
    r1 = cp(4, gx.at[3, lo], gx.at[2, lo], right)
    l0.wait_recv()
    l1 = cp(5, gx.at[1, hi], gx.at[2, hi], left)
    r1.wait_recv()
    l1.wait_recv()

    def weigh(base, h):
        return sum(w(base + d, h) * gx[d, h].astype(F32) for d in range(4))

    for h in range(part):
        hout[h] = weigh(2, h).astype(BF16)
    z0 = cp(6, hout, hin, zp)
    c1.wait_recv()
    z0.wait_recv()
    for h in range(part):
        eout[h] = (weigh(6, h) + w(10, h) * hin[h].astype(F32)).astype(BF16)
    e0 = cp(7, eout, ein, mate)

    def finish(start, e):
        for h in range(part):
            row = pl.ds(start + h, 1)
            out_ref[start + h] = (
                w_ref[12, row, :] * theirs[start + h].astype(F32)
                + w_ref[11, row, :] * e[h].astype(F32)
            )

    finish(first, eout)
    e0.wait_recv()
    finish((1 - core) * part, ein)
    for copy in (c0, c1, r0, l0, r1, l1, z0, e0):
        copy.wait_send()


def prefix_ctx(s, logs, cid):
    me = lax.axis_index("ctx")
    heads = s.shape[0]
    core, x, zh = lax.rem(me, 2), lax.rem(me // 2, 4), me // 8
    four = logs.reshape(2, 4, 2, heads)
    chip = four.sum(axis=2)
    own = lax.dynamic_index_in_dim(chip, zh, 0, keepdims=False)
    run = jnp.cumsum(own, axis=0)
    before = run - own
    first_log = four[zh, x, 0]
    one = jnp.ones((heads,), F32)
    zero = jnp.zeros((heads,), F32)
    rows = [
        jnp.where(core == 0, one, jnp.exp(first_log)),
        jnp.where(core == 0, jnp.exp(first_log), one),
    ]
    for d in range(4):
        rows.append(jnp.exp(before[lax.rem(x + d, 4)]))
    for d in range(4):
        at = lax.rem(x + d, 4)
        rows.append(jnp.where(at > x, jnp.exp(jnp.minimum(before[at] - run[x], 0.0)), zero))
    rows.append(jnp.where(zh == 0, jnp.exp(run[3] - run[x]), zero))
    rows.append(jnp.where(core == 0, jnp.exp(four[zh, x, 1]), one))
    rows.append(jnp.where(core == 0, one, zero))
    weights = jnp.broadcast_to(jnp.stack(rows)[:, :, None], (13, heads, 128))
    part = (heads // 2,) + s.shape[1:]
    return pl.pallas_call(
        prefix_kernel,
        out_shape=jax.ShapeDtypeStruct(s.shape, F32),
        in_specs=[VM, VM],
        out_specs=VM,
        scratch_shapes=[
            pltpu.VMEM(s.shape, BF16),
            pltpu.VMEM(s.shape, BF16),
            pltpu.VMEM((4,) + part, BF16),
            pltpu.VMEM(part, BF16),
            pltpu.VMEM(part, BF16),
            pltpu.VMEM(part, BF16),
            pltpu.VMEM(part, BF16),
            pltpu.SemaphoreType.DMA((8,)),
            pltpu.SemaphoreType.DMA((8,)),
        ],
        compiler_params=params(cid),
        name="prefix_ctx",
    )(s, weights)


def contract_last(left, right):
    return lax.dot_general(
        left, right, (((1,), (1,)), ((), ())), preferred_element_type=jnp.float32
    )


def split_three(value):
    a = value.astype(BF16)
    rest = value - a.astype(F32)
    b = rest.astype(BF16)
    return a, b, (rest - b.astype(F32)).astype(BF16)


def on_device(
    hidden_in,
    upstream,
    query_ckpt,
    keyval_ckpt,
    attn_out_grad,
    segments,
    query_weight,
    keyval_weight,
    mix_weight,
    out_weight,
    state_in_ckpt,
    state_out_ckpt,
    step_size,
    decay_rate,
    skip_gain,
):
    local_rows, width_part = upstream.shape
    head_size = keyval_ckpt.shape[1] // 2
    query_heads = query_ckpt.shape[1] // head_size
    mamba_heads = step_size.shape[1]
    scaling = head_size ** (-0.5)
    log_step = -decay_rate[None, :] * step_size
    cumulative = jnp.cumsum(log_step, axis=0)
    block_log = cumulative[-1]
    mixed = jnp.dot(
        lax.all_gather(hidden_in, "tp", axis=1, tiled=True),
        mix_weight,
        preferred_element_type=jnp.float32,
    ).astype(jnp.bfloat16)
    first_row = lax.axis_index("ctx") * local_rows
    tail = jnp.pad(
        jnp.stack(split_three(block_log)), ((0, 13), (0, 2 * head_size - mamba_heads))
    )
    gathered = gather_ctx(jnp.concatenate([keyval_ckpt, tail], axis=0), 1)
    logs = gathered[:, local_rows : local_rows + 3, :mamba_heads].astype(F32)
    logs = logs[:, 0] + logs[:, 1] + logs[:, 2]
    keyval_all = gathered[:, :local_rows].reshape(-1, 2 * head_size)
    total_rows = keyval_all.shape[0]
    key_rows = keyval_all[:, :head_size]
    value_rows = keyval_all[:, head_size:]
    query_segs = lax.dynamic_slice_in_dim(segments, first_row, local_rows)
    query_pos = first_row + jnp.arange(local_rows, dtype=jnp.int32)
    key_pos = jnp.arange(total_rows, dtype=jnp.int32)
    allowed = (key_pos[None, :] <= query_pos[:, None]) & (segments[None, :] == query_segs[:, None])
    grad_list = []
    score_list = []
    weight_list = []
    for head_index in range(query_heads):
        query_rows = query_ckpt[:, head_index * head_size : (head_index + 1) * head_size]
        grad_rows = attn_out_grad[:, head_index * head_size : (head_index + 1) * head_size]
        scores = contract_last(query_rows, key_rows) * scaling
        scores = jnp.where(allowed, scores, -jnp.inf)
        row_max = jnp.max(scores, axis=1, keepdims=True)
        exponent = jnp.where(allowed, jnp.exp(scores - row_max), 0.0)
        softmax = exponent / jnp.sum(exponent, axis=1, keepdims=True)
        weights_b = softmax.astype(jnp.bfloat16)
        output = jnp.dot(weights_b, value_rows, preferred_element_type=jnp.float32)
        correction = jnp.sum(grad_rows.astype(jnp.float32) * output, axis=1, keepdims=True)
        prob_grad = contract_last(grad_rows, value_rows)
        score_grad = (softmax * (prob_grad - correction) * scaling).astype(jnp.bfloat16)
        grad_list.append(jnp.dot(score_grad, key_rows, preferred_element_type=jnp.float32))
        score_list.append(score_grad)
        weight_list.append(weights_b)
    query_grad = jnp.concatenate(grad_list, axis=1).astype(jnp.bfloat16)
    score_all = jnp.stack(score_list)
    weight_all = jnp.stack(weight_list)
    query_three = query_ckpt.reshape(local_rows, query_heads, head_size)
    grad_three = attn_out_grad.reshape(local_rows, query_heads, head_size)
    key_part = jnp.einsum("hqk,qhe->ke", score_all, query_three, preferred_element_type=jnp.float32)
    value_part = jnp.einsum(
        "hqk,qhe->ke", weight_all, grad_three, preferred_element_type=jnp.float32
    )
    keyval_part = jnp.concatenate([key_part, value_part], axis=1).astype(jnp.bfloat16)
    keyval_grad = scatter_ctx(keyval_part.reshape(2, 4, 2, local_rows, 2 * head_size), 2)

    def owners(weight):
        return weight.reshape(8, width_part, weight.shape[1])

    def to_owners(left, weight):
        return jnp.einsum("te,kfe->ktf", left, owners(weight), preferred_element_type=jnp.float32)

    attn_partial = to_owners(query_grad, query_weight) + to_owners(keyval_grad, keyval_weight)
    grad_mid = scatter_tp(attn_partial.astype(jnp.bfloat16), upstream, 3)
    mid_all = gather_tp(grad_mid, 4)
    mix_out_grad = jnp.einsum(
        "ktf,mkf->tm",
        mid_all,
        out_weight.reshape(-1, 8, width_part),
        preferred_element_type=jnp.float32,
    ).astype(jnp.bfloat16)
    inner_size = mixed.shape[1] // mamba_heads
    later_mask = (jnp.arange(local_rows)[None, :] >= jnp.arange(local_rows)[:, None])[None]
    spread = cumulative.T[:, None, :] - cumulative.T[:, :, None]
    decay_mat = jnp.where(later_mask, jnp.exp(jnp.where(later_mask, spread, 0.0)), 0.0)
    grad_float = mix_out_grad.reshape(local_rows, mamba_heads, inner_size).astype(jnp.float32)
    mixed_float = mixed.reshape(local_rows, mamba_heads, inner_size).astype(jnp.float32)
    in_float = state_in_ckpt.astype(jnp.float32)
    out_float = state_out_ckpt.astype(jnp.float32)
    inner_bc = contract_last(state_in_ckpt, state_out_ckpt)
    contribution = jnp.einsum(
        "thp,tn->hpn", grad_float * jnp.exp(cumulative)[:, :, None], out_float, precision=HIGH
    )
    carried_in = prefix_ctx(contribution, logs, 5)
    to_end = jnp.exp(block_log[None, :] - cumulative)[:, :, None]
    local_part = jnp.einsum("hst,thp->shp", inner_bc[None] * decay_mat, grad_float, precision=HIGH)
    carried = jnp.einsum("sn,hpn->shp", in_float, carried_in, precision=HIGH) * to_end
    mixed_grad = (
        (step_size[:, :, None] * (local_part + carried) + skip_gain[None, :, None] * grad_float)
        .astype(jnp.bfloat16)
        .reshape(local_rows, mamba_heads * inner_size)
    )
    pair_mat = jnp.einsum("shp,thp->hst", mixed_float, grad_float, precision=HIGH) * decay_mat
    state_local = jnp.einsum("hst,tn->shn", pair_mat, out_float, precision=HIGH)
    state_carried = jnp.einsum("shp,hpn->shn", mixed_float, carried_in, precision=HIGH) * to_end
    grad_state_in = jnp.sum(step_size[:, :, None] * (state_local + state_carried), axis=1)
    ssm_partial = to_owners(mixed_grad, mix_weight).astype(jnp.bfloat16)
    grad_hidden = scatter_tp(ssm_partial, grad_mid, 6)
    return (grad_mid, grad_hidden, grad_state_in)


def solution(mesh):
    placed = (
        P("ctx", "tp"),
        P("ctx", "tp"),
        P("ctx", "tp"),
        P("ctx", "tp"),
        P("ctx", "tp"),
        P(),
        P(None, "tp"),
        P(None, "tp"),
        P(None, "tp"),
        P("tp", None),
        P("ctx", "tp"),
        P("ctx", "tp"),
        P("ctx", "tp"),
        P("tp"),
        P("tp"),
    )
    return jax.shard_map(
        on_device,
        mesh=mesh,
        in_specs=placed,
        out_specs=(P("ctx", "tp"), P("ctx", "tp"), P("ctx", "tp")),
        check_vma=False,
    )
```

```python
import jax
import jax.numpy as jnp
from jax import lax
from jax.experimental import pallas as pl
from jax.experimental.pallas import tpu as pltpu
from jax.sharding import PartitionSpec as P

HIGH = lax.Precision.HIGHEST
MESH = pl.DeviceIdType.MESH
VM = pl.BlockSpec(memory_space=pltpu.VMEM)
F32 = jnp.float32
BF16 = jnp.bfloat16


def remote(src, dst, send, recv, to):
    return pltpu.make_async_remote_copy(
        src_ref=src, dst_ref=dst, send_sem=send, recv_sem=recv, device_id=to, device_id_type=MESH
    )


def greet(peers):
    barrier = pltpu.get_barrier_semaphore()
    for peer in peers:
        pl.semaphore_signal(barrier, inc=1, device_id=peer, device_id_type=MESH)
    pl.semaphore_wait(barrier, len(peers))


def params(cid, mib=40):
    return pltpu.CompilerParams(
        collective_id=cid, has_side_effects=True, vmem_limit_bytes=mib << 20
    )


def tp_places():
    c = lax.axis_index("ctx")
    me = lax.axis_index("tp")
    zp = me + 1 - 2 * lax.rem(me, 2)
    return c, me, zp, lax.rem(me + 2, 8), lax.rem(me + 6, 8)


def ctx_places():
    tp = lax.axis_index("tp")
    me = lax.axis_index("ctx")
    core = lax.rem(me, 2)
    x = lax.rem(me // 2, 4)
    zh = me // 8

    def at(z, place, c):
        return z * 8 + lax.rem(place, 4) * 2 + c

    return tp, me, core, x, zh, at


def dot(left, right, over, precision=None):
    return lax.dot_general(
        left,
        right,
        (((over[0],), (over[1],)), ((), ())),
        preferred_element_type=F32,
        precision=precision,
    )


def lower(n):
    row = lax.broadcasted_iota(jnp.int32, (n, n), 0)
    col = lax.broadcasted_iota(jnp.int32, (n, n), 1)
    return (col <= row).astype(F32)

def gather_ctx_kernel(kv_ref, step_ref, decay_ref, out_ref, cum_ref, cumt_ref, x_ref, ssem, rsem, lsem):
    rows = kv_ref.shape[0]
    log_step = -decay_ref[...] * step_ref[...]
    cum_ref[...] = dot(lower(rows), log_step, (1, 0), HIGH)
    cumt_ref[...] = dot(log_step, lower(rows), (0, 1), HIGH)
    x_ref[pl.ds(0, rows)] = kv_ref[...]
    pad = jnp.zeros((16, x_ref.shape[1] - step_ref.shape[1]), F32)
    line = lax.broadcasted_iota(jnp.int32, x_ref[pl.ds(0, 16)].shape, 0)
    total = jnp.concatenate([jnp.broadcast_to(cum_ref[pl.ds(rows - 1, 1)], (16, step_ref.shape[1])), pad], axis=1)
    a = total.astype(BF16).astype(F32)
    b = (total - a).astype(BF16).astype(F32)
    c = total - a - b
    x_ref[pl.ds(rows, 16)] = jnp.where(
        line == 0, a, jnp.where(line == 1, b, jnp.where(line == 2, c, 0.0))
    ).astype(BF16)
    tp, me, core, x, zh, at = ctx_places()
    mate = at(zh, x, 1 - core)
    right, left = at(zh, x + 1, core), at(zh, x + 3, core)
    zp = at(1 - zh, x, core)
    half = x_ref.shape[0] // 2
    lo, hi = pl.ds(0, half), pl.ds(half, half)
    greet([(mate, tp), (right, tp), (left, tp), (zp, tp)])
    sent = []

    def cp(k, slot, to, part=None, own=False):
        dst = out_ref.at[slot] if part is None else out_ref.at[slot, part]
        copy = remote(x_ref if own else dst, dst, ssem.at[k], rsem.at[k], (to, tp))
        copy.start()
        sent.append(copy)
        return copy

    z0 = cp(0, me, zp, own=True)
    r0 = cp(1, me, right, own=True)
    l0 = cp(2, me, left, own=True)
    m = [cp(3, me, mate, own=True)]
    mine = pltpu.make_async_copy(x_ref, out_ref.at[me], lsem)
    mine.start()
    fr = []
    k = 4
    for z, direct in ((zh, (r0, l0)), (1 - zh, None)):
        if direct is None:
            z0.wait_recv()
            direct = (cp(k, zp, right), cp(k + 1, zp, left))
            m.append(cp(k + 2, zp, mate))
            k += 3
        direct[0].wait_recv()
        fr.append((z, cp(k, at(z, x + 3, core), right, lo)))
        m.append(cp(k + 1, at(z, x + 3, core), mate))
        direct[1].wait_recv()
        fr.append((z, cp(k + 2, at(z, x + 1, core), left, hi)))
        m.append(cp(k + 3, at(z, x + 1, core), mate))
        k += 4
    for part, (z, copy) in zip((lo, hi, lo, hi), fr):
        copy.wait_recv()
        m.append(cp(k, at(z, x + 2, core), mate, part))
        k += 1
    for copy in m:
        copy.wait_recv()
    for copy in sent:
        copy.wait_send()
    mine.wait()


def gather_ctx(x, step, decay, cid):
    rows, cols = x.shape
    heads = step.shape[1]
    rows += 16
    return pl.pallas_call(
        gather_ctx_kernel,
        out_shape=(
            jax.ShapeDtypeStruct((16, rows, cols), x.dtype),
            jax.ShapeDtypeStruct(step.shape, F32),
            jax.ShapeDtypeStruct((heads, step.shape[0]), F32),
        ),
        in_specs=[VM] * 3,
        out_specs=(VM,) * 3,
        scratch_shapes=[
            pltpu.VMEM((rows, cols), BF16),
            pltpu.SemaphoreType.DMA((19,)),
            pltpu.SemaphoreType.DMA((19,)),
            pltpu.SemaphoreType.DMA,
        ],
        compiler_params=params(cid),
        name="gather_ctx",
    )(x, step, decay)


def scatter_ctx_kernel(p_ref, out_ref, got, uin, vin, zin, tout, uout, zout, ssem, rsem):
    tp, me, core, x, zh, at = ctx_places()
    mate = at(zh, x, 1 - core)
    right, left = at(zh, x + 1, core), at(zh, x + 3, core)
    zp = at(1 - zh, x, core)
    half = out_ref.shape[0] // 2
    lo, hi = pl.ds(0, half), pl.ds(half, half)
    greet([(mate, tp), (right, tp), (left, tp), (zp, tp)])

    def cp(k, src, dst, to):
        copy = remote(src, dst, ssem.at[k], rsem.at[k], (to, tp))
        copy.start()
        return copy

    g = {}
    for k, d in enumerate((2, 1, 3, 0)):
        g[d] = cp(k, p_ref.at[:, lax.rem(x + d, 4), 1 - core], got.at[d], mate)

    def both(d):
        g[d].wait_recv()
        return p_ref[:, lax.rem(x + d, 4), core].astype(F32) + got[d].astype(F32)

    tout[...] = both(2).astype(BF16)
    t0 = cp(4, tout.at[:, lo], uin.at[0], right)
    t1 = cp(5, tout.at[:, hi], uin.at[1], left)
    q = both(1)
    t0.wait_recv()
    uout[0, :, lo] = (q[:, :half] + uin[0].astype(F32)).astype(BF16)
    uout[0, :, hi] = q[:, half:].astype(BF16)
    u0 = cp(6, uout.at[0], vin.at[0], right)
    q = both(3)
    t1.wait_recv()
    uout[1, :, hi] = (q[:, half:] + uin[1].astype(F32)).astype(BF16)
    uout[1, :, lo] = q[:, :half].astype(BF16)
    u1 = cp(7, uout.at[1], vin.at[1], left)
    g[0].wait_recv()
    u0.wait_recv()
    u1.wait_recv()

    def total(z):
        return (
            p_ref[z, x, core].astype(F32)
            + got[0, z].astype(F32)
            + vin[0, z].astype(F32)
            + vin[1, z].astype(F32)
        )

    zout[...] = total(1 - zh).astype(BF16)
    zc = cp(8, zout, zin, zp)
    mine = total(zh)
    zc.wait_recv()
    out_ref[...] = (mine + zin[...].astype(F32)).astype(BF16)
    for copy in (g[0], g[1], g[2], g[3], t0, t1, u0, u1, zc):
        copy.wait_send()


def scatter_ctx(p, cid):
    rows, cols = p.shape[-2:]
    two = (2, rows, cols)
    return pl.pallas_call(
        scatter_ctx_kernel,
        out_shape=jax.ShapeDtypeStruct((rows, cols), BF16),
        in_specs=[VM],
        out_specs=VM,
        scratch_shapes=[
            pltpu.VMEM((4,) + two, BF16),
            pltpu.VMEM((2, 2, rows // 2, cols), BF16),
            pltpu.VMEM((2,) + two, BF16),
            pltpu.VMEM((rows, cols), BF16),
            pltpu.VMEM(two, BF16),
            pltpu.VMEM((2,) + two, BF16),
            pltpu.VMEM((rows, cols), BF16),
            pltpu.SemaphoreType.DMA((9,)),
            pltpu.SemaphoreType.DMA((9,)),
        ],
        compiler_params=params(cid),
        name="scatter_ctx",
    )(p)


def attention_kernel(bound_ref, q_ref, g_ref, kv_ref, dq_ref, dkv_ref, s_ref, q4, g4, most, ol, dq4, t4, d4):
    rows, width = q_ref.shape
    size = kv_ref.shape[2] // 2
    heads = width // size
    scaling = size ** (-0.5)
    me = lax.axis_index("ctx")
    bound = bound_ref[0]
    first = jnp.where(me * rows >= bound, bound // rows, 0)
    dkv_ref[...] = jnp.zeros_like(dkv_ref)
    for h in range(heads):
        q4[h] = q_ref[:, h * size : (h + 1) * size]
        g4[h] = g_ref[:, h * size : (h + 1) * size]
    most[...] = jnp.full_like(most, -jnp.inf)
    ol[...] = jnp.zeros_like(ol)
    dq4[...] = jnp.zeros_like(dq4)

    def twice(a):
        return jnp.concatenate([a, a], axis=1)

    def scores(j, _):
        k = kv_ref[j, :rows, :size]
        q_pos = me * rows + lax.broadcasted_iota(jnp.int32, (rows, rows), 0)
        k_pos = j * rows + lax.broadcasted_iota(jnp.int32, (rows, rows), 1)
        start = jnp.where(q_pos >= bound, bound, 0)
        bias = jnp.where((k_pos <= q_pos) & (k_pos >= start), 0.0, -1e30)
        for h in range(heads):
            s = dot(q4[h], k, (1, 1)) + bias
            s_ref[j, h] = s
            most[h] = jnp.maximum(most[h], jnp.maximum(s[:, :size], s[:, size:]))
        return 0

    lax.fori_loop(first, me + 1, scores, 0)
    for h in range(heads):
        most[h] = jnp.broadcast_to(jnp.max(most[h], axis=1, keepdims=True), (rows, size))

    def weigh(j, _):
        v = jnp.concatenate([kv_ref[j, :rows, size:], jnp.ones((rows, size), BF16)], axis=1)
        for h in range(heads):
            p = jnp.exp((s_ref[j, h] - twice(most[h])) * scaling)
            s_ref[j, h] = p
            ol[h] += dot(p.astype(BF16), v, (1, 0))
        return 0

    lax.fori_loop(first, me + 1, weigh, 0)
    for h in range(heads):
        inverse = 1.0 / ol[h, :, size:]
        out = ol[h, :, :size] * inverse
        corr = jnp.sum(out * g4[h].astype(F32), axis=1, keepdims=True)
        ol[h, :, :size] = jnp.broadcast_to(corr, (rows, size))
        ol[h, :, size:] = inverse

    def grads(j, _):
        k = kv_ref[j, :rows, :size]
        v = kv_ref[j, :rows, size:]
        for h in range(heads):
            t = s_ref[j, h] * twice(ol[h, :, size:])
            d = (t * (dot(g4[h], v, (1, 1)) - twice(ol[h, :, :size]))).astype(BF16)
            t4[h] = t.astype(BF16)
            d4[h] = d
            dq4[h] += dot(d, k, (1, 0))
        dk = dot(d4[...].reshape(heads * rows, rows), q4[...].reshape(heads * rows, size), (0, 0))
        dv = dot(t4[...].reshape(heads * rows, rows), g4[...].reshape(heads * rows, size), (0, 0))
        dkv_ref[j] = jnp.concatenate([dk * scaling, dv], axis=1).astype(BF16)
        return 0

    lax.fori_loop(first, me + 1, grads, 0)
    for h in range(heads):
        dq_ref[:, h * size : (h + 1) * size] = (dq4[h] * scaling).astype(BF16)


def attention(bound, query, grad, keyval):
    blocks, _, cols = keyval.shape
    rows, width = query.shape
    size = cols // 2
    heads = width // size
    return pl.pallas_call(
        attention_kernel,
        out_shape=(
            jax.ShapeDtypeStruct(query.shape, BF16),
            jax.ShapeDtypeStruct((blocks, rows, cols), BF16),
        ),
        in_specs=[pl.BlockSpec(memory_space=pltpu.SMEM), VM, VM, VM],
        out_specs=(VM, VM),
        scratch_shapes=[
            pltpu.VMEM((blocks, heads, rows, rows), F32),
            pltpu.VMEM((heads, rows, size), BF16),
            pltpu.VMEM((heads, rows, size), BF16),
            pltpu.VMEM((heads, rows, size), F32),
            pltpu.VMEM((heads, rows, 2 * size), F32),
            pltpu.VMEM((heads, rows, size), F32),
            pltpu.VMEM((heads, rows, rows), BF16),
            pltpu.VMEM((heads, rows, rows), BF16),
        ],
        compiler_params=pltpu.CompilerParams(vmem_limit_bytes=48 << 20),
        name="attention",
    )(bound, query, grad, keyval)


def sent_sums(term, add, buf, base, ssem, rsem, beside):
    c, me, zp, up, down = tp_places()
    opp = lax.rem(me + 4, 8)

    def other(k):
        return k + 1 - 2 * lax.rem(k, 2)

    tin, uin, win, vin, out = buf
    half = tin.shape[0] // 2
    lo, hi = pl.ds(0, half), pl.ds(half, half)
    copies = []

    def cp(k, src, dst, to):
        copy = remote(src, dst, ssem.at[base + k], rsem.at[base + k], (c, to))
        copy.start()
        copies.append(copy)
        return copy

    out[0] = term(other(opp)).astype(BF16)
    a = cp(0, out.at[0], tin, zp)
    out[1] = term(other(up)).astype(BF16)
    w0 = cp(1, out.at[1], win.at[0], up)
    out[2] = term(other(down)).astype(BF16)
    w1 = cp(2, out.at[2], win.at[1], down)
    held = term(opp)
    a.wait_recv()
    out[3] = (held + tin[...].astype(F32)).astype(BF16)
    t0 = cp(3, out.at[3, lo], uin.at[0], up)
    t1 = cp(4, out.at[3, hi], uin.at[1], down)
    held = term(zp)
    w0.wait_recv()
    w1.wait_recv()
    out[4] = (held + win[0].astype(F32) + win[1].astype(F32)).astype(BF16)
    v = cp(5, out.at[4], vin, zp)
    held = term(up)
    out[5, hi] = held[half:].astype(BF16)
    t0.wait_recv()
    out[5, lo] = (held[:half] + uin[0].astype(F32)).astype(BF16)
    u0 = cp(6, out.at[5], win.at[2], up)
    held = term(down)
    out[6, lo] = held[:half].astype(BF16)
    t1.wait_recv()
    out[6, hi] = (held[half:] + uin[1].astype(F32)).astype(BF16)
    u1 = cp(7, out.at[6], win.at[3], down)
    held = term(me) + add()
    beside()
    v.wait_recv()
    u0.wait_recv()
    u1.wait_recv()
    result = held + vin[...].astype(F32) + win[2].astype(F32) + win[3].astype(F32)
    for copy in copies:
        copy.wait_send()
    return result


def spread_out(mine, everyone, base, ssem, rsem, use):
    c, me, zp, up, down = tp_places()
    opp = lax.rem(me + 4, 8)

    def other(k):
        return k + 1 - 2 * lax.rem(k, 2)

    half = everyone.shape[1] // 2
    lo, hi = pl.ds(0, half), pl.ds(half, half)
    copies = []

    def cp(k, slot, to, part=None):
        ref = everyone.at[slot] if part is None else everyone.at[slot, part]
        copy = remote(ref, ref, ssem.at[base + k], rsem.at[base + k], (c, to))
        copy.start()
        copies.append(copy)
        return copy

    everyone[me] = mine
    c1 = cp(1, me, up)
    c2 = cp(2, me, down)
    c0 = cp(0, me, zp)
    use(me)
    c1.wait_recv()
    c5 = cp(5, down, up, lo)
    c2.wait_recv()
    c6 = cp(6, up, down, hi)
    c0.wait_recv()
    c3 = cp(3, zp, up)
    c4 = cp(4, zp, down)
    use(down)
    c5.wait_recv()
    c7 = cp(7, opp, zp, lo)
    use(up)
    c6.wait_recv()
    c8 = cp(8, opp, zp, hi)
    use(zp)
    use(opp)
    c3.wait_recv()
    use(other(down))
    c4.wait_recv()
    use(other(up))
    c7.wait_recv()
    c8.wait_recv()
    use(other(opp))
    for copy in copies:
        copy.wait_send()


def prefix_weights(logs, heads):
    tp, me, core, x, zh, at = ctx_places()
    j = lax.broadcasted_iota(jnp.int32, (16, 128), 0)
    jz, jx, jc = j // 8, lax.rem(j // 2, 4), lax.rem(j, 2)

    def factor(mask, scale):
        log = dot(logs, jnp.where(mask, 1.0, 0.0), (0, 0), HIGH)
        return jnp.exp(log) * scale

    one = jnp.float32(1.0)
    zero = jnp.float32(0.0)
    same = (jz == zh) & (jx == x)
    rows = [
        factor(same & (jc + 1 == core), one),
        factor(same & (jc + core == 0), one),
    ]
    for d in range(4):
        rows.append(factor((jz == zh) & (jx < lax.rem(x + d, 4)), one))
    for d in range(4):
        to = lax.rem(x + d, 4)
        rows.append(
            factor((jz == zh) & (jx > x) & (jx < to), jnp.where(to > x, one, zero))
        )
    rows.append(factor((jz == 0) & (jx > x), jnp.where(zh == 0, one, zero)))
    rows.append(factor(same & (jc == core + 1), one))
    rows.append(jnp.full((heads, 128), jnp.where(core == 0, one, zero)))
    return rows


def tail_kernel(
    qg_ref, kvg_ref, up_ref, qw_hbm, kw_hbm, ow_hbm, mw_hbm, hid_ref, b_ref, c_ref, cum_ref, cumt_ref,
    step_ref, skip_ref, logs_ref,
    mid_ref, hidden_ref, state_ref,
    qw, kw, ow, mw, tin, uin, win, vin, out, tin2, uin2, win2, vin2, out2, everyone, y_acc, y, mixed,
    local, pairs, w_ref, s_ref, mine, theirs, gx, hout, hin, eout, ein, carried, ssem, rsem, lsem,
):
    rows, width = up_ref.shape
    heads = step_ref.shape[1]
    inner = mixed.shape[1]
    size = inner // heads
    tp, me, core, x, zh, at = ctx_places()
    c, tme, tzp, tup, tdown = tp_places()
    mate = at(zh, x, 1 - core)
    right, left = at(zh, x + 1, core), at(zh, x + 3, core)
    zp = at(1 - zh, x, core)
    loads = [
        pltpu.make_async_copy(src, dst, lsem.at[k])
        for k, (src, dst) in enumerate(((qw_hbm, qw), (kw_hbm, kw), (ow_hbm, ow), (mw_hbm, mw)))
    ]
    for load in loads:
        load.start()
    greet(
        [(c, tzp), (c, tup), (c, tdown), (mate, tp), (right, tp), (left, tp), (zp, tp)]
    )

    def part(k):
        return pl.ds(pl.multiple_of(k * width, width), width)

    for k, value in enumerate(prefix_weights(logs_ref[...], heads)):
        w_ref[k] = value
    loads[0].wait()
    loads[1].wait()

    def attn_term(k):
        return dot(qg_ref[...], qw[part(k)], (1, 1)) + dot(kvg_ref[...], kw[part(k)], (1, 1))

    def mix():
        loads[3].wait()

        def step(k, _):
            y_acc[...] += dot(hid_ref[:, part(k)], mw[part(k)], (1, 0))
            return 0

        y_acc[...] = jnp.zeros_like(y_acc)
        lax.fori_loop(0, 8, step, 0)
        mixed[...] = y_acc[...].astype(BF16)

    mid = sent_sums(
        attn_term, lambda: up_ref[...].astype(F32), (tin, uin, win, vin, out), 0, ssem, rsem, mix
    ).astype(BF16)
    mid_ref[...] = mid
    loads[2].wait()
    y_acc[...] = jnp.zeros_like(y_acc)

    def out_term(k):
        y_acc[...] += dot(everyone[k], ow[:, part(k)], (1, 1))

    spread_out(mid, everyone, 8, ssem, rsem, out_term)
    y[...] = y_acc[...].astype(BF16)

    spot = lax.broadcasted_iota(jnp.int32, (heads, inner), 1)
    head = lax.broadcasted_iota(jnp.int32, (heads, inner), 0) * size
    wide = jnp.where((spot >= head) & (spot < head + size), 1.0, 0.0).astype(BF16)

    def widen(value):
        high = value.astype(BF16)
        low = (value - high.astype(F32)).astype(BF16)
        return dot(high, wide, (1, 0)) + dot(low, wide, (1, 0))

    cum = cum_ref[...]
    weighted = (y[...].astype(F32) * widen(jnp.exp(cum))).astype(BF16)
    s_ref[...] = dot(weighted, c_ref[...], (0, 0)).reshape(s_ref.shape)
    count = heads // 2
    first = core * count
    half = count // 2
    lo, hi = pl.ds(0, half), pl.ds(half, half)
    other = pl.ds((1 - core) * count, count)
    ours = pl.ds(first, count)
    copies = []

    def cp(k, src, dst, to):
        copy = remote(src, dst, ssem.at[17 + k], rsem.at[17 + k], (to, tp))
        copy.start()
        copies.append(copy)
        return copy

    mine[...] = s_ref[...].astype(BF16)
    c0 = cp(0, mine.at[other], theirs.at[other], mate)
    c1 = cp(1, mine.at[ours], theirs.at[ours], mate)

    def w(k, h):
        return w_ref[k, pl.ds(first + h, 1), :]

    inner_bc = dot(b_ref[...], c_ref[...], (1, 1))
    line = lax.broadcasted_iota(jnp.int32, (rows, rows), 0)
    col = lax.broadcasted_iota(jnp.int32, (rows, rows), 1)
    later = col >= line
    left_lane = lax.broadcasted_iota(jnp.int32, (rows, 2 * size), 1) < size

    def decay(h):
        spread = cumt_ref[pl.ds(h, 1), :] - cum_ref[:, h : h + 1]
        return jnp.exp(jnp.where(later, spread, -1e30))

    def pair_of(ref, p):
        both = ref[:, p * 2 * size : (p + 1) * 2 * size]
        none = jnp.zeros_like(both)
        return jnp.where(left_lane, both, none), jnp.where(left_lane, none, both), both

    def local_pairs(start, stop):
        for p in range(start, stop):
            y0, y1, _ = pair_of(y, p)
            a0 = (inner_bc * decay(2 * p)).astype(BF16)
            a1 = (inner_bc * decay(2 * p + 1)).astype(BF16)
            local[:, p * 2 * size : (p + 1) * 2 * size] = dot(a0, y0, (1, 0)) + dot(a1, y1, (1, 0))

    c0.wait_recv()
    for h in range(count):
        gx[0, h] = (
            w(0, h) * s_ref[first + h] + w(1, h) * theirs[first + h].astype(F32)
        ).astype(BF16)
    r0 = cp(2, gx.at[0], gx.at[3], right)
    l0 = cp(3, gx.at[0], gx.at[1], left)
    local_pairs(0, 3)
    r0.wait_recv()
    r1 = cp(4, gx.at[3, lo], gx.at[2, lo], right)
    l0.wait_recv()
    l1 = cp(5, gx.at[1, hi], gx.at[2, hi], left)
    local_pairs(3, 5)
    r1.wait_recv()
    l1.wait_recv()

    def weigh(base, h):
        return sum(w(base + d, h) * gx[d, h].astype(F32) for d in range(4))

    for h in range(count):
        hout[h] = weigh(2, h).astype(BF16)
    z0 = cp(6, hout, hin, zp)
    local_pairs(5, 8)
    c1.wait_recv()
    z0.wait_recv()
    for h in range(count):
        eout[h] = (weigh(6, h) + w(10, h) * hin[h].astype(F32)).astype(BF16)
    e0 = cp(7, eout, ein, mate)

    def finish(start, e):
        for h in range(count):
            row = pl.ds(start + h, 1)
            carried[start + h] = (
                w_ref[12, row, :] * theirs[start + h].astype(F32)
                + w_ref[11, row, :] * e[h].astype(F32)
            ).astype(BF16)

    finish(first, eout)
    ending = widen(jnp.exp(cum_ref[pl.ds(rows - 1, 1)] - cum))
    stepping = widen(step_ref[...])
    skipping = widen(jnp.broadcast_to(skip_ref[...], (rows, heads)))
    e0.wait_recv()
    finish((1 - core) * count, ein)
    state = carried[...].reshape(inner, s_ref.shape[2])
    y_float = y[...].astype(F32)
    grad_in = (
        stepping * (local[...] + dot(b_ref[...], state, (1, 1)) * ending) + skipping * y_float
    ).astype(BF16)
    y_acc[...] = stepping * ending

    def mix_term(k):
        return dot(grad_in, mw[part(k)], (1, 1))

    def states():
        scaled = (mixed[...].astype(F32) * y_acc[...]).astype(BF16)
        pairs[...] = jnp.zeros_like(pairs)
        for p in range(heads // 2):
            m0, m1, _ = pair_of(mixed, p)
            both = y[:, p * 2 * size : (p + 1) * 2 * size]
            for h, m in ((2 * p, m0), (2 * p + 1, m1)):
                pairs[...] += dot(m, both, (1, 1)) * decay(h) * step_ref[:, h : h + 1]
        state_ref[...] = dot(pairs[...].astype(BF16), c_ref[...], (1, 0)) + dot(
            scaled, state, (1, 0)
        )

    hidden_ref[...] = sent_sums(
        mix_term, lambda: mid_ref[...].astype(F32), (tin2, uin2, win2, vin2, out2), 25, ssem, rsem, states
    ).astype(BF16)
    for copy in copies:
        copy.wait_send()


def tail(query_grad, keyval_grad, upstream, weights, hidden_all, b, c, cum, cumt, step, skip, logs, cid):
    rows, width = upstream.shape
    inner = weights[3].shape[1]
    heads = step.shape[1]
    full = (rows, width)
    state = (heads, inner // heads, b.shape[1])
    part = (heads // 2,) + state[1:]
    any_spec = pl.BlockSpec(memory_space=pl.ANY)

    def sums():
        return [
            pltpu.VMEM(full, BF16),
            pltpu.VMEM((2, rows // 2, width), BF16),
            pltpu.VMEM((4,) + full, BF16),
            pltpu.VMEM(full, BF16),
            pltpu.VMEM((7,) + full, BF16),
        ]

    return pl.pallas_call(
        tail_kernel,
        out_shape=(
            jax.ShapeDtypeStruct(full, BF16),
            jax.ShapeDtypeStruct(full, BF16),
            jax.ShapeDtypeStruct((rows, b.shape[1]), F32),
        ),
        in_specs=[VM] * 3 + [any_spec] * 4 + [VM] * 8,
        out_specs=(VM,) * 3,
        scratch_shapes=[pltpu.VMEM(weight.shape, BF16) for weight in weights]
        + sums()
        + sums()
        + [
            pltpu.VMEM((8,) + full, BF16),
            pltpu.VMEM((rows, inner), F32),
            pltpu.VMEM((rows, inner), BF16),
            pltpu.VMEM((rows, inner), BF16),
            pltpu.VMEM((rows, inner), F32),
            pltpu.VMEM((rows, rows), F32),
            pltpu.VMEM((13, heads, 128), F32),
            pltpu.VMEM(state, F32),
            pltpu.VMEM(state, BF16),
            pltpu.VMEM(state, BF16),
            pltpu.VMEM((4,) + part, BF16),
            pltpu.VMEM(part, BF16),
            pltpu.VMEM(part, BF16),
            pltpu.VMEM(part, BF16),
            pltpu.VMEM(part, BF16),
            pltpu.VMEM(state, BF16),
            pltpu.SemaphoreType.DMA((33,)),
            pltpu.SemaphoreType.DMA((33,)),
            pltpu.SemaphoreType.DMA((4,)),
        ],
        compiler_params=params(cid, 58),
        name="tail",
    )(query_grad, keyval_grad, upstream, *weights, hidden_all, b, c, cum, cumt, step, skip, logs)


def on_device(
    hidden_in,
    upstream,
    query_ckpt,
    keyval_ckpt,
    attn_out_grad,
    segments,
    query_weight,
    keyval_weight,
    mix_weight,
    out_weight,
    state_in_ckpt,
    state_out_ckpt,
    step_size,
    decay_rate,
    skip_gain,
):
    rows = upstream.shape[0]
    cols = keyval_ckpt.shape[1]
    heads = step_size.shape[1]
    hidden_all = lax.all_gather(hidden_in, "tp", axis=1, tiled=True)
    gathered, cum, cumt = gather_ctx(keyval_ckpt, step_size, decay_rate[None, :], 1)
    logs = gathered[:, rows : rows + 3, :heads].astype(F32).sum(axis=1)
    bound = jnp.sum((segments == 0).astype(jnp.int32))[None]
    query_grad, keyval_part = attention(bound, query_ckpt, attn_out_grad, gathered)
    keyval_grad = scatter_ctx(keyval_part.reshape(2, 4, 2, rows, cols), 2)
    return tail(
        query_grad,
        keyval_grad,
        upstream,
        (query_weight, keyval_weight, out_weight, mix_weight),
        hidden_all,
        state_in_ckpt,
        state_out_ckpt,
        cum,
        cumt,
        step_size,
        skip_gain[None, :],
        logs,
        3,
    )


def solution(mesh):
    placed = (
        P("ctx", "tp"),
        P("ctx", "tp"),
        P("ctx", "tp"),
        P("ctx", "tp"),
        P("ctx", "tp"),
        P(),
        P(None, "tp"),
        P(None, "tp"),
        P(None, "tp"),
        P("tp", None),
        P("ctx", "tp"),
        P("ctx", "tp"),
        P("ctx", "tp"),
        P("tp"),
        P("tp"),
    )
    return jax.shard_map(
        on_device,
        mesh=mesh,
        in_specs=placed,
        out_specs=(P("ctx", "tp"), P("ctx", "tp"), P("ctx", "tp")),
        check_vma=False,
    )
```

```python
import jax
import jax.numpy as jnp
from jax import lax
from jax.experimental import pallas as pl
from jax.experimental.pallas import tpu as pltpu
from jax.sharding import PartitionSpec as P

HIGH = lax.Precision.HIGHEST
MESH = pl.DeviceIdType.MESH
VM = pl.BlockSpec(memory_space=pltpu.VMEM)
F32 = jnp.float32
BF16 = jnp.bfloat16


def remote(src, dst, send, recv, to):
    return pltpu.make_async_remote_copy(
        src_ref=src, dst_ref=dst, send_sem=send, recv_sem=recv, device_id=to, device_id_type=MESH
    )


def greet(peers):
    barrier = pltpu.get_barrier_semaphore()
    for peer in peers:
        pl.semaphore_signal(barrier, inc=1, device_id=peer, device_id_type=MESH)
    pl.semaphore_wait(barrier, len(peers))


def params(cid, mib=40):
    return pltpu.CompilerParams(
        collective_id=cid, has_side_effects=True, vmem_limit_bytes=mib << 20
    )


def tp_places():
    c = lax.axis_index("ctx")
    me = lax.axis_index("tp")
    zp = me + 1 - 2 * lax.rem(me, 2)
    return c, me, zp, lax.rem(me + 2, 8), lax.rem(me + 6, 8)


def ctx_places():
    tp = lax.axis_index("tp")
    me = lax.axis_index("ctx")
    core = lax.rem(me, 2)
    x = lax.rem(me // 2, 4)
    zh = me // 8

    def at(z, place, c):
        return z * 8 + lax.rem(place, 4) * 2 + c

    return tp, me, core, x, zh, at


def dot(left, right, over, precision=None):
    return lax.dot_general(
        left,
        right,
        (((over[0],), (over[1],)), ((), ())),
        preferred_element_type=F32,
        precision=precision,
    )


def lower(n):
    row = lax.broadcasted_iota(jnp.int32, (n, n), 0)
    col = lax.broadcasted_iota(jnp.int32, (n, n), 1)
    return (col <= row).astype(F32)


def sent_sums(term, add, buf, base, ssem, rsem, beside):
    c, me, zp, up, down = tp_places()
    opp = lax.rem(me + 4, 8)

    def other(k):
        return k + 1 - 2 * lax.rem(k, 2)

    tin, uin, win, vin, out = buf
    half = tin.shape[0] // 2
    lo, hi = pl.ds(0, half), pl.ds(half, half)
    copies = []

    def cp(k, src, dst, to):
        copy = remote(src, dst, ssem.at[base + k], rsem.at[base + k], (c, to))
        copy.start()
        copies.append(copy)
        return copy

    out[0] = term(other(opp)).astype(BF16)
    a = cp(0, out.at[0], tin, zp)
    out[1] = term(other(up)).astype(BF16)
    w0 = cp(1, out.at[1], win.at[0], up)
    out[2] = term(other(down)).astype(BF16)
    w1 = cp(2, out.at[2], win.at[1], down)
    held = term(opp)
    a.wait_recv()
    out[3] = (held + tin[...].astype(F32)).astype(BF16)
    t0 = cp(3, out.at[3, lo], uin.at[0], up)
    t1 = cp(4, out.at[3, hi], uin.at[1], down)
    held = term(zp)
    w0.wait_recv()
    w1.wait_recv()
    out[4] = (held + win[0].astype(F32) + win[1].astype(F32)).astype(BF16)
    v = cp(5, out.at[4], vin, zp)
    held = term(up)
    out[5, hi] = held[half:].astype(BF16)
    t0.wait_recv()
    out[5, lo] = (held[:half] + uin[0].astype(F32)).astype(BF16)
    u0 = cp(6, out.at[5], win.at[2], up)
    held = term(down)
    out[6, lo] = held[:half].astype(BF16)
    t1.wait_recv()
    out[6, hi] = (held[half:] + uin[1].astype(F32)).astype(BF16)
    u1 = cp(7, out.at[6], win.at[3], down)
    held = term(me) + add()
    beside()
    v.wait_recv()
    u0.wait_recv()
    u1.wait_recv()
    result = held + vin[...].astype(F32) + win[2].astype(F32) + win[3].astype(F32)
    for copy in copies:
        copy.wait_send()
    return result


def spread_out(mine, everyone, base, ssem, rsem, use):
    c, me, zp, up, down = tp_places()
    opp = lax.rem(me + 4, 8)

    def other(k):
        return k + 1 - 2 * lax.rem(k, 2)

    half = everyone.shape[1] // 2
    lo, hi = pl.ds(0, half), pl.ds(half, half)
    copies = []

    def cp(k, slot, to, part=None):
        ref = everyone.at[slot] if part is None else everyone.at[slot, part]
        copy = remote(ref, ref, ssem.at[base + k], rsem.at[base + k], (c, to))
        copy.start()
        copies.append(copy)
        return copy

    everyone[me] = mine
    c1 = cp(1, me, up)
    c2 = cp(2, me, down)
    c0 = cp(0, me, zp)
    use(me)
    c1.wait_recv()
    c5 = cp(5, down, up, lo)
    c2.wait_recv()
    c6 = cp(6, up, down, hi)
    c0.wait_recv()
    c3 = cp(3, zp, up)
    c4 = cp(4, zp, down)
    use(down)
    c5.wait_recv()
    c7 = cp(7, opp, zp, lo)
    use(up)
    c6.wait_recv()
    c8 = cp(8, opp, zp, hi)
    use(zp)
    use(opp)
    c3.wait_recv()
    use(other(down))
    c4.wait_recv()
    use(other(up))
    c7.wait_recv()
    c8.wait_recv()
    use(other(opp))
    for copy in copies:
        copy.wait_send()


def prefix_weights(logs, heads):
    tp, me, core, x, zh, at = ctx_places()
    j = lax.broadcasted_iota(jnp.int32, (16, 128), 0)
    jz, jx, jc = j // 8, lax.rem(j // 2, 4), lax.rem(j, 2)

    def factor(mask, scale):
        log = dot(logs, jnp.where(mask, 1.0, 0.0), (0, 0), HIGH)
        return jnp.exp(log) * scale

    one = jnp.float32(1.0)
    zero = jnp.float32(0.0)
    same = (jz == zh) & (jx == x)
    rows = [
        factor(same & (jc + 1 == core), one),
        factor(same & (jc + core == 0), one),
    ]
    for d in range(4):
        rows.append(factor((jz == zh) & (jx < lax.rem(x + d, 4)), one))
    for d in range(4):
        to = lax.rem(x + d, 4)
        rows.append(
            factor((jz == zh) & (jx > x) & (jx < to), jnp.where(to > x, one, zero))
        )
    rows.append(factor((jz == 0) & (jx > x), jnp.where(zh == 0, one, zero)))
    rows.append(factor(same & (jc == core + 1), one))
    rows.append(jnp.full((heads, 128), jnp.where(core == 0, one, zero)))
    return rows


def whole_kernel(
    kv_hbm, q_hbm, g_hbm, hid_hbm, qw_hbm, kw_hbm, ow_hbm, mw_hbm, up_hbm, b_hbm, c_hbm,
    step_ref, decay_ref, seg_ref, skip_ref,
    mid_ref, hidden_ref, state_ref,
    kv, kvall, s_ref, q4, g4, most, ol, dq4, t4, d4, p,
    got, uin, vin, zin, tout, uout, zout, dq_ref, kvg_ref, hid, cum_ref, cumt_ref, steps, logs,
    qw, kw, ow, mw, up_ref, b_ref, c_ref, tin, tuin, rin, rv, rout, everyone, y_acc, y, mixed,
    local, pairs, w_ref, terms, ours_out, theirs, gx, hout, hin, eout, ein, carried,
    ssem, rsem, hssem, hrsem, tssem, trsem, lsem,
):
    tp, me, core, x, zh, at = ctx_places()
    c, tme, tzp, tup, tdown = tp_places()
    topp = lax.rem(tme + 4, 8)
    mate = at(zh, x, 1 - core)
    right, left, opp = at(zh, x + 1, core), at(zh, x + 3, core), at(zh, x + 2, core)
    zp = at(1 - zh, x, core)
    heads, rows, size = q4.shape
    scaling = size ** (-0.5)
    own_rows = pl.ds(0, rows)
    loads = [pltpu.make_async_copy(kv_hbm, kv.at[own_rows], lsem.at[0])]
    hid_own = pltpu.make_async_copy(hid_hbm, hid.at[tme], lsem.at[1])
    weights = [
        pltpu.make_async_copy(src, dst, lsem.at[2 + k])
        for k, (src, dst) in enumerate(((qw_hbm, qw), (kw_hbm, kw), (ow_hbm, ow), (mw_hbm, mw)))
    ]
    more = [
        pltpu.make_async_copy(src, dst, lsem.at[6 + k])
        for k, (src, dst) in enumerate(((up_hbm, up_ref), (b_hbm, b_ref), (c_hbm, c_ref)))
    ]
    for h in range(heads):
        lanes = pl.ds(h * size, size)
        loads.append(pltpu.make_async_copy(q_hbm.at[:, lanes], q4.at[h], lsem.at[9 + h]))
        loads.append(pltpu.make_async_copy(g_hbm.at[:, lanes], g4.at[h], lsem.at[9 + heads + h]))
    loads[0].start()
    hid_own.start()
    for load in loads[1:] + weights + more:
        load.start()
    barrier = pltpu.get_barrier_semaphore()
    peers = [(c, tzp), (c, tup), (c, tdown), (mate, tp), (right, tp), (left, tp), (zp, tp)]
    for peer in peers:
        pl.semaphore_signal(barrier, inc=1, device_id=peer, device_id_type=MESH)

    groups = step_ref.shape[0]
    tri = lower(rows)
    eye = jnp.where(
        lax.broadcasted_iota(jnp.int32, (groups, groups), 0)
        == lax.broadcasted_iota(jnp.int32, (groups, groups), 1),
        -decay_ref[...],
        0.0,
    )
    log_step = dot(eye, step_ref[...], (1, 0), HIGH)
    cum_ref[...] = dot(tri, log_step, (1, 1), HIGH)
    cumt_ref[...] = dot(log_step, tri, (1, 1), HIGH)
    row = lax.broadcasted_iota(jnp.int32, (rows, rows), 0)
    col = lax.broadcasted_iota(jnp.int32, (rows, rows), 1)
    steps[...] = dot(jnp.where(row == col, 1.0, 0.0), step_ref[...], (1, 1), HIGH)
    pad = jnp.zeros((16, 2 * size - groups), F32)
    total = jnp.concatenate(
        [jnp.broadcast_to(cum_ref[pl.ds(rows - 1, 1)], (16, groups)), pad], axis=1
    )
    line = lax.broadcasted_iota(jnp.int32, total.shape, 0)
    one = total.astype(BF16).astype(F32)
    two = (total - one).astype(BF16).astype(F32)
    kv[pl.ds(rows, 16)] = jnp.where(
        line == 0, one, jnp.where(line == 1, two, jnp.where(line == 2, total - one - two, 0.0))
    ).astype(BF16)
    seg = jnp.where(seg_ref[...] == 0, 1.0, 0.0)
    bound = jnp.sum(jnp.sum(seg, axis=1, keepdims=True), axis=0, keepdims=True)
    loads[0].wait()
    pl.semaphore_wait(barrier, len(peers))

    sent = []

    def cp(k, slot, to, part=None, own=False):
        dst = kvall.at[slot] if part is None else kvall.at[slot, part]
        copy = remote(kv if own else dst, dst, ssem.at[k], rsem.at[k], (to, tp))
        copy.start()
        sent.append(copy)
        return copy

    def hp(k, slot, to, part=None):
        dst = hid.at[slot] if part is None else hid.at[slot, part]
        copy = remote(dst, dst, hssem.at[k], hrsem.at[k], (c, to))
        copy.start()
        sent.append(copy)
        return copy

    lo, hi = pl.ds(0, 128), pl.ds(128, kv.shape[0] - 128)
    z0 = cp(0, me, zp, own=True)
    r0 = cp(1, me, right, own=True)
    l0 = cp(2, me, left, own=True)
    m0 = cp(3, me, mate, own=True)
    mine = pltpu.make_async_copy(kv, kvall.at[me], lsem.at[0])
    mine.start()
    hid_own.wait()
    h0 = hp(0, tme, tzp)
    h1 = hp(1, tme, tup)
    h2 = hp(2, tme, tdown)

    most[...] = jnp.full_like(most, -jnp.inf)
    ol[...] = jnp.zeros_like(ol)
    dq4[...] = jnp.zeros_like(dq4)
    p[...] = jnp.zeros_like(p)
    reach = 3 * 4096 // (4 * rows)
    first = jnp.maximum(me - reach, 0)
    for load in loads[1:]:
        load.wait()
    q_pos = (me * rows + row).astype(F32)
    floor = jnp.where(q_pos >= bound, bound, 0.0)

    def twice(a):
        return jnp.concatenate([a, a], axis=1)

    def scores(j):
        @pl.when((j <= me) & (j >= first))
        def _():
            k = kvall[j, :rows, :size]
            k_pos = (j * rows + col).astype(F32)
            bias = jnp.where((k_pos <= q_pos) & (k_pos >= floor), 0.0, -1e30)
            for h in range(heads):
                s = dot(q4[h], k, (1, 1)) + bias
                s_ref[j - first, h] = s
                most[h] = jnp.maximum(most[h], jnp.maximum(s[:, :size], s[:, size:]))

    mine.wait()
    scores(me)
    m0.wait_recv()
    scores(mate)
    r0.wait_recv()
    f1 = cp(4, left, right, lo)
    m1 = cp(5, left, mate)
    l0.wait_recv()
    f2 = cp(6, right, left, hi)
    m2 = cp(7, right, mate)
    z0.wait_recv()
    zr = cp(8, zp, right)
    zl = cp(9, zp, left)
    m3 = cp(10, zp, mate)
    scores(left)
    scores(right)
    f1.wait_recv()
    m4 = cp(11, opp, mate, lo)
    f2.wait_recv()
    m5 = cp(12, opp, mate, hi)
    scores(zp)
    zright, zleft, zopp = at(1 - zh, x + 1, core), at(1 - zh, x + 3, core), at(1 - zh, x + 2, core)
    zr.wait_recv()
    f3 = cp(13, zleft, right, lo)
    m6 = cp(14, zleft, mate)
    zl.wait_recv()
    f4 = cp(15, zright, left, hi)
    m7 = cp(16, zright, mate)
    scores(opp)
    m1.wait_recv()
    scores(at(zh, x + 3, 1 - core))
    m2.wait_recv()
    scores(at(zh, x + 1, 1 - core))
    m3.wait_recv()
    scores(at(1 - zh, x, 1 - core))
    f3.wait_recv()
    m8 = cp(17, zopp, mate, lo)
    f4.wait_recv()
    m9 = cp(18, zopp, mate, hi)
    scores(zleft)
    scores(zright)
    m4.wait_recv()
    m5.wait_recv()
    scores(at(zh, x + 2, 1 - core))
    m6.wait_recv()
    scores(at(1 - zh, x + 3, 1 - core))
    m7.wait_recv()
    scores(at(1 - zh, x + 1, 1 - core))
    scores(zopp)
    m8.wait_recv()
    m9.wait_recv()
    scores(at(1 - zh, x + 2, 1 - core))

    h0.wait_recv()
    h1.wait_recv()
    h2.wait_recv()
    h5 = hp(5, tdown, tup, pl.ds(0, 128))
    h6 = hp(6, tup, tdown, pl.ds(128, 128))
    h3 = hp(3, tzp, tup)
    h4 = hp(4, tzp, tdown)

    logs[...] = (
        kvall[:, rows, :groups].astype(F32)
        + kvall[:, rows + 1, :groups].astype(F32)
        + kvall[:, rows + 2, :groups].astype(F32)
    )
    for h in range(heads):
        most[h] = jnp.broadcast_to(jnp.max(most[h], axis=1, keepdims=True), (rows, size))

    def weigh(j, _):
        v = jnp.concatenate([kvall[j, :rows, size:], jnp.ones((rows, size), BF16)], axis=1)
        for h in range(heads):
            e = jnp.exp((s_ref[j - first, h] - twice(most[h])) * scaling)
            s_ref[j - first, h] = e
            ol[h] += dot(e.astype(BF16), v, (1, 0))
        return 0

    lax.fori_loop(first, me + 1, weigh, 0)
    for h in range(heads):
        inverse = 1.0 / ol[h, :, size:]
        out = ol[h, :, :size] * inverse
        corr = jnp.sum(out * g4[h].astype(F32), axis=1, keepdims=True)
        ol[h, :, :size] = jnp.broadcast_to(corr, (rows, size))
        ol[h, :, size:] = inverse

    h5.wait_recv()
    h7 = hp(7, topp, tzp, pl.ds(0, 128))
    h6.wait_recv()
    h8 = hp(8, topp, tzp, pl.ds(128, 128))

    def grads(place, c_at):
        def one_z(z, _):
            j = at(z, place, c_at)

            @pl.when((j <= me) & (j >= first))
            def _():
                k = kvall[j, :rows, :size]
                v = kvall[j, :rows, size:]
                for h in range(heads):
                    t = s_ref[j - first, h] * twice(ol[h, :, size:])
                    d = (t * (dot(g4[h], v, (1, 1)) - twice(ol[h, :, :size]))).astype(BF16)
                    t4[h] = t.astype(BF16)
                    d4[h] = d
                    dq4[h] += dot(d, k, (1, 0))
                dk = dot(d4[...].reshape(heads * rows, rows), q4[...].reshape(heads * rows, size), (0, 0))
                dv = dot(t4[...].reshape(heads * rows, rows), g4[...].reshape(heads * rows, size), (0, 0))
                p[z, lax.rem(place, 4), c_at] = jnp.concatenate([dk * scaling, dv], axis=1).astype(BF16)

            return 0

        lax.fori_loop(0, 2, one_z, 0)

    half = rows // 2
    low, high = pl.ds(0, half), pl.ds(half, half)

    def sp(k, src, dst, to):
        copy = remote(src, dst, ssem.at[19 + k], rsem.at[19 + k], (to, tp))
        copy.start()
        sent.append(copy)
        return copy

    def to_mate(k, d):
        grads(x + d, 1 - core)
        return sp(k, p.at[:, lax.rem(x + d, 4), 1 - core], got.at[d], mate)

    def both(d):
        return p[:, lax.rem(x + d, 4), core].astype(F32) + got[d].astype(F32)

    g2 = to_mate(0, 2)
    grads(x + 2, core)
    g1 = to_mate(1, 1)
    g2.wait_recv()
    tout[...] = both(2).astype(BF16)
    t0 = sp(4, tout.at[:, low], uin.at[0], right)
    t1 = sp(5, tout.at[:, high], uin.at[1], left)
    grads(x + 1, core)
    g3 = to_mate(2, 3)
    g1.wait_recv()
    t0.wait_recv()
    u = both(1)
    uout[0, :, low] = (u[:, :half] + uin[0].astype(F32)).astype(BF16)
    uout[0, :, high] = u[:, half:].astype(BF16)
    u0 = sp(6, uout.at[0], vin.at[0], right)
    grads(x + 3, core)
    g3.wait_recv()
    t1.wait_recv()
    u = both(3)
    uout[1, :, high] = (u[:, half:] + uin[1].astype(F32)).astype(BF16)
    uout[1, :, low] = u[:, :half].astype(BF16)
    u1 = sp(7, uout.at[1], vin.at[1], left)
    g0 = to_mate(3, 0)
    grads(x, core)
    for h in range(heads):
        dq_ref[:, h * size : (h + 1) * size] = (dq4[h] * scaling).astype(BF16)
    g0.wait_recv()
    u0.wait_recv()
    u1.wait_recv()

    def whole(z):
        return (
            p[z, x, core].astype(F32)
            + got[0, z].astype(F32)
            + vin[0, z].astype(F32)
            + vin[1, z].astype(F32)
        )

    zout[...] = whole(1 - zh).astype(BF16)
    zc = sp(8, zout, zin, zp)
    kept = whole(zh)
    zc.wait_recv()
    kvg_ref[...] = (kept + zin[...].astype(F32)).astype(BF16)
    h3.wait_recv()
    h4.wait_recv()
    h7.wait_recv()
    h8.wait_recv()
    for copy in sent:
        copy.wait_send()

    width = up_ref.shape[1]
    inner = mixed.shape[1]
    state_size = inner // groups

    def part(k):
        return pl.ds(pl.multiple_of(k * width, width), width)

    for index, value in enumerate(prefix_weights(logs[...], groups)):
        w_ref[index] = value
    weights[0].wait()
    weights[1].wait()
    for load in more:
        load.wait()

    def attn_term(k):
        return dot(dq_ref[...], qw[part(k)], (1, 1)) + dot(kvg_ref[...], kw[part(k)], (1, 1))

    def mix():
        weights[3].wait()

        def step(k, _):
            y_acc[...] += dot(hid[k], mw[part(k)], (1, 0))
            return 0

        y_acc[...] = jnp.zeros_like(y_acc)
        lax.fori_loop(0, 8, step, 0)
        mixed[...] = y_acc[...].astype(BF16)

    mid = sent_sums(
        attn_term, lambda: up_ref[...].astype(F32), (tin, tuin, rin, rv, rout), 0, tssem, trsem, mix
    ).astype(BF16)
    mid_ref[...] = mid
    weights[2].wait()
    y_acc[...] = jnp.zeros_like(y_acc)

    def out_term(k):
        y_acc[...] += dot(everyone[k], ow[:, part(k)], (1, 1))

    spread_out(mid, everyone, 8, tssem, trsem, out_term)
    y[...] = y_acc[...].astype(BF16)

    spot = lax.broadcasted_iota(jnp.int32, (groups, inner), 1)
    head = lax.broadcasted_iota(jnp.int32, (groups, inner), 0) * state_size
    wide = jnp.where((spot >= head) & (spot < head + state_size), 1.0, 0.0).astype(BF16)

    def widen(value):
        high = value.astype(BF16)
        low = (value - high.astype(F32)).astype(BF16)
        return dot(high, wide, (1, 0)) + dot(low, wide, (1, 0))

    cum = cum_ref[...]
    weighted = (y[...].astype(F32) * widen(jnp.exp(cum))).astype(BF16)
    terms[...] = dot(weighted, c_ref[...], (0, 0)).reshape(terms.shape)
    count = groups // 2
    begin = core * count
    half = count // 2
    lo, hi = pl.ds(0, half), pl.ds(half, half)
    theirs_at = pl.ds((1 - core) * count, count)
    ours = pl.ds(begin, count)
    copies = []

    def pp(k, src, dst, to):
        copy = remote(src, dst, tssem.at[17 + k], trsem.at[17 + k], (to, tp))
        copy.start()
        copies.append(copy)
        return copy

    ours_out[...] = terms[...].astype(BF16)
    c0 = pp(0, ours_out.at[theirs_at], theirs.at[theirs_at], mate)
    c1 = pp(1, ours_out.at[ours], theirs.at[ours], mate)

    def w(k, h):
        return w_ref[k, pl.ds(begin + h, 1), :]

    inner_bc = dot(b_ref[...], c_ref[...], (1, 1))
    later = col >= row
    left_lane = lax.broadcasted_iota(jnp.int32, (rows, 2 * state_size), 1) < state_size

    def decay(h):
        spread = cumt_ref[pl.ds(h, 1), :] - cum_ref[:, h : h + 1]
        return jnp.exp(jnp.where(later, spread, -1e30))

    def pair_of(ref, p):
        both = ref[:, p * 2 * state_size : (p + 1) * 2 * state_size]
        none = jnp.zeros_like(both)
        return jnp.where(left_lane, both, none), jnp.where(left_lane, none, both), both

    def local_pairs(start, stop):
        for p in range(start, stop):
            y0, y1, _ = pair_of(y, p)
            a0 = (inner_bc * decay(2 * p)).astype(BF16)
            a1 = (inner_bc * decay(2 * p + 1)).astype(BF16)
            local[:, p * 2 * state_size : (p + 1) * 2 * state_size] = dot(a0, y0, (1, 0)) + dot(a1, y1, (1, 0))

    c0.wait_recv()
    for h in range(count):
        gx[0, h] = (
            w(0, h) * terms[begin + h] + w(1, h) * theirs[begin + h].astype(F32)
        ).astype(BF16)
    r0 = pp(2, gx.at[0], gx.at[3], right)
    l0 = pp(3, gx.at[0], gx.at[1], left)
    local_pairs(0, 3)
    r0.wait_recv()
    r1 = pp(4, gx.at[3, lo], gx.at[2, lo], right)
    l0.wait_recv()
    l1 = pp(5, gx.at[1, hi], gx.at[2, hi], left)
    local_pairs(3, 5)
    r1.wait_recv()
    l1.wait_recv()

    def weigh(base, h):
        return sum(w(base + d, h) * gx[d, h].astype(F32) for d in range(4))

    for h in range(count):
        hout[h] = weigh(2, h).astype(BF16)
    z0 = pp(6, hout, hin, zp)
    local_pairs(5, 8)
    c1.wait_recv()
    z0.wait_recv()
    for h in range(count):
        eout[h] = (weigh(6, h) + w(10, h) * hin[h].astype(F32)).astype(BF16)
    e0 = pp(7, eout, ein, mate)

    def finish(start, e):
        for h in range(count):
            at_h = pl.ds(start + h, 1)
            carried[start + h] = (
                w_ref[12, at_h, :] * theirs[start + h].astype(F32)
                + w_ref[11, at_h, :] * e[h].astype(F32)
            ).astype(BF16)

    finish(begin, eout)
    ending = widen(jnp.exp(cum_ref[pl.ds(rows - 1, 1)] - cum))
    stepping = widen(steps[...])
    skipping = widen(jnp.broadcast_to(skip_ref[...], (rows, groups)))
    e0.wait_recv()
    finish((1 - core) * count, ein)
    state = carried[...].reshape(inner, terms.shape[2])
    y_float = y[...].astype(F32)
    grad_in = (
        stepping * (local[...] + dot(b_ref[...], state, (1, 1)) * ending) + skipping * y_float
    ).astype(BF16)
    y_acc[...] = stepping * ending

    def mix_term(k):
        return dot(grad_in, mw[part(k)], (1, 1))

    def states():
        scaled = (mixed[...].astype(F32) * y_acc[...]).astype(BF16)
        pairs[...] = jnp.zeros_like(pairs)
        for p in range(groups // 2):
            m0, m1, _ = pair_of(mixed, p)
            both = y[:, p * 2 * state_size : (p + 1) * 2 * state_size]
            for h, m in ((2 * p, m0), (2 * p + 1, m1)):
                pairs[...] += dot(m, both, (1, 1)) * decay(h) * steps[:, h : h + 1]
        state_ref[...] = dot(pairs[...].astype(BF16), c_ref[...], (1, 0)) + dot(
            scaled, state, (1, 0)
        )

    hidden_ref[...] = sent_sums(
        mix_term, lambda: mid_ref[...].astype(F32), (tin, tuin, rin, rv, rout), 25, tssem, trsem, states
    ).astype(BF16)
    for copy in copies:
        copy.wait_send()


def whole(arrays, cid):
    keyval, query, _, hidden, qw, kw, ow, mw, upstream, b, c, step = arrays[:12]
    rows, cols = keyval.shape
    size = cols // 2
    heads = query.shape[1] // size
    groups = step.shape[0]
    inner = mw.shape[1]
    full = upstream.shape
    state = (groups, inner // groups, b.shape[1])
    part = (groups // 2,) + state[1:]
    any_spec = pl.BlockSpec(memory_space=pl.ANY)
    two = (2, rows, cols)
    vm = pltpu.VMEM
    dma = pltpu.SemaphoreType.DMA
    return pl.pallas_call(
        whole_kernel,
        out_shape=(
            jax.ShapeDtypeStruct(full, BF16),
            jax.ShapeDtypeStruct(full, BF16),
            jax.ShapeDtypeStruct((rows, b.shape[1]), F32),
        ),
        in_specs=[any_spec] * 11 + [VM] * 4,
        out_specs=(VM,) * 3,
        scratch_shapes=[
            vm((rows + 16, cols), BF16),
            vm((16, rows + 16, cols), BF16),
            vm((13, heads, rows, rows), F32),
            vm((heads, rows, size), BF16),
            vm((heads, rows, size), BF16),
            vm((heads, rows, size), F32),
            vm((heads, rows, 2 * size), F32),
            vm((heads, rows, size), F32),
            vm((heads, rows, rows), BF16),
            vm((heads, rows, rows), BF16),
            vm((2, 4, 2, rows, cols), BF16),
            vm((4,) + two, BF16),
            vm((2, 2, rows // 2, cols), BF16),
            vm((2,) + two, BF16),
            vm((rows, cols), BF16),
            vm(two, BF16),
            vm((2,) + two, BF16),
            vm((rows, cols), BF16),
            vm(query.shape, BF16),
            vm(keyval.shape, BF16),
            vm((8,) + hidden.shape, BF16),
            vm((rows, groups), F32),
            vm((groups, rows), F32),
            vm((rows, groups), F32),
            vm((16, groups), F32),
            vm(qw.shape, BF16),
            vm(kw.shape, BF16),
            vm(ow.shape, BF16),
            vm(mw.shape, BF16),
            vm(full, BF16),
            vm(b.shape, BF16),
            vm(c.shape, BF16),
            vm(full, BF16),
            vm((2, rows // 2, full[1]), BF16),
            vm((4,) + full, BF16),
            vm(full, BF16),
            vm((7,) + full, BF16),
            vm((8,) + full, BF16),
            vm((rows, inner), F32),
            vm((rows, inner), BF16),
            vm((rows, inner), BF16),
            vm((rows, inner), F32),
            vm((rows, rows), F32),
            vm((13, groups, 128), F32),
            vm(state, F32),
            vm(state, BF16),
            vm(state, BF16),
            vm((4,) + part, BF16),
            vm(part, BF16),
            vm(part, BF16),
            vm(part, BF16),
            vm(part, BF16),
            vm(state, BF16),
            dma((28,)),
            dma((28,)),
            dma((9,)),
            dma((9,)),
            dma((33,)),
            dma((33,)),
            dma((17,)),
        ],
        compiler_params=pltpu.CompilerParams(
            collective_id=cid, has_side_effects=True, vmem_limit_bytes=(64 << 20) - (256 << 10)
        ),
        name="whole",
    )(*arrays)


def finish_kernel(a_ref, b_ref, c_ref, a_out, b_out, c_out):
    a_out[...] = a_ref[...]
    b_out[...] = b_ref[...]
    c_out[...] = c_ref[...]


def finish(arrays):
    return pl.pallas_call(
        finish_kernel,
        out_shape=tuple(jax.ShapeDtypeStruct(a.shape, a.dtype) for a in arrays),
        in_specs=[VM] * 3,
        out_specs=(VM,) * 3,
        name="finish",
    )(*arrays)


def on_device(
    hidden_in,
    upstream,
    query_ckpt,
    keyval_ckpt,
    attn_out_grad,
    segments,
    query_weight,
    keyval_weight,
    mix_weight,
    out_weight,
    state_in_ckpt,
    state_out_ckpt,
    step_size,
    decay_rate,
    skip_gain,
):
    return finish(
        whole(
            (
                keyval_ckpt,
                query_ckpt,
                attn_out_grad,
                hidden_in,
                query_weight,
                keyval_weight,
                out_weight,
                mix_weight,
                upstream,
                state_in_ckpt,
                state_out_ckpt,
                step_size.T,
                decay_rate[None, :],
                segments.reshape(-1, 128),
                skip_gain[None, :],
            ),
            1,
        )
    )


def solution(mesh):
    placed = (
        P("ctx", "tp"),
        P("ctx", "tp"),
        P("ctx", "tp"),
        P("ctx", "tp"),
        P("ctx", "tp"),
        P(),
        P(None, "tp"),
        P(None, "tp"),
        P(None, "tp"),
        P("tp", None),
        P("ctx", "tp"),
        P("ctx", "tp"),
        P("ctx", "tp"),
        P("tp"),
        P("tp"),
    )
    return jax.shard_map(
        on_device,
        mesh=mesh,
        in_specs=placed,
        out_specs=(P("ctx", "tp"), P("ctx", "tp"), P("ctx", "tp")),
        check_vma=False,
    )
```

```python
import jax
import jax.numpy as jnp
from jax import lax
from jax.experimental import pallas as pl
from jax.experimental.pallas import tpu as pltpu
from jax.sharding import PartitionSpec as P

HIGH = lax.Precision.HIGHEST
MESH = pl.DeviceIdType.MESH
VM = pl.BlockSpec(memory_space=pltpu.VMEM)
F32 = jnp.float32
BF16 = jnp.bfloat16


def remote(src, dst, send, recv, to):
    return pltpu.make_async_remote_copy(
        src_ref=src, dst_ref=dst, send_sem=send, recv_sem=recv, device_id=to, device_id_type=MESH
    )


def greet(peers):
    barrier = pltpu.get_barrier_semaphore()
    for peer in peers:
        pl.semaphore_signal(barrier, inc=1, device_id=peer, device_id_type=MESH)
    pl.semaphore_wait(barrier, len(peers))


def params(cid, mib=40):
    return pltpu.CompilerParams(
        collective_id=cid, has_side_effects=True, vmem_limit_bytes=mib << 20
    )


def tp_places():
    c = lax.axis_index("ctx")
    me = lax.axis_index("tp")
    zp = me + 1 - 2 * lax.rem(me, 2)
    return c, me, zp, lax.rem(me + 2, 8), lax.rem(me + 6, 8)


def ctx_places():
    tp = lax.axis_index("tp")
    me = lax.axis_index("ctx")
    core = lax.rem(me, 2)
    x = lax.rem(me // 2, 4)
    zh = me // 8

    def at(z, place, c):
        return z * 8 + lax.rem(place, 4) * 2 + c

    return tp, me, core, x, zh, at


def dot(left, right, over, precision=None):
    return lax.dot_general(
        left,
        right,
        (((over[0],), (over[1],)), ((), ())),
        preferred_element_type=F32,
        precision=precision,
    )


def lower(n):
    row = lax.broadcasted_iota(jnp.int32, (n, n), 0)
    col = lax.broadcasted_iota(jnp.int32, (n, n), 1)
    return (col <= row).astype(F32)


def sent_sums(term, add, buf, base, ssem, rsem, beside):
    c, me, zp, up, down = tp_places()
    opp = lax.rem(me + 4, 8)

    def other(k):
        return k + 1 - 2 * lax.rem(k, 2)

    tin, uin, win, vin, out = buf
    half = tin.shape[0] // 2
    lo, hi = pl.ds(0, half), pl.ds(half, half)
    copies = []

    def cp(k, src, dst, to):
        copy = remote(src, dst, ssem.at[base + k], rsem.at[base + k], (c, to))
        copy.start()
        copies.append(copy)
        return copy

    out[0] = term(other(opp)).astype(BF16)
    a = [cp(n, out.at[0, part], tin.at[part], zp) for n, part in enumerate((lo, hi))]
    out[1] = term(other(up)).astype(BF16)
    w0 = [cp(2, out.at[1, lo], win.at[0, lo], up)]
    out[2] = term(other(down)).astype(BF16)
    w1 = [cp(3, out.at[2, lo], win.at[1, lo], down)]
    w0.append(cp(4, out.at[1, hi], win.at[0, hi], up))
    w1.append(cp(5, out.at[2, hi], win.at[1, hi], down))
    to_up = term(up)
    out[5, hi] = to_up[half:].astype(BF16)
    to_down = term(down)
    out[6, lo] = to_down[:half].astype(BF16)
    held = term(opp)
    a[0].wait_recv()
    out[3, lo] = (held[:half] + tin[lo].astype(F32)).astype(BF16)
    t0 = cp(6, out.at[3, lo], uin.at[0], up)
    u0 = [cp(8, out.at[5, hi], win.at[2, hi], up)]
    u1 = [cp(9, out.at[6, lo], win.at[3, lo], down)]
    a[1].wait_recv()
    out[3, hi] = (held[half:] + tin[hi].astype(F32)).astype(BF16)
    t1 = cp(7, out.at[3, hi], uin.at[1], down)
    held = term(zp)
    v = []
    for n, part in enumerate((lo, hi)):
        w0[n].wait_recv()
        w1[n].wait_recv()
        rows = slice(n * half, (n + 1) * half)
        out[4, part] = (
            held[rows] + win[0, part].astype(F32) + win[1, part].astype(F32)
        ).astype(BF16)
        v.append(cp(10 + n, out.at[4, part], vin.at[part], zp))
    t0.wait_recv()
    out[5, lo] = (to_up[:half] + uin[0].astype(F32)).astype(BF16)
    u0.append(cp(12, out.at[5, lo], win.at[2, lo], up))
    t1.wait_recv()
    out[6, hi] = (to_down[half:] + uin[1].astype(F32)).astype(BF16)
    u1.append(cp(13, out.at[6, hi], win.at[3, hi], down))
    held = term(me) + add()
    beside()
    for copy in v + u0 + u1:
        copy.wait_recv()
    result = held + vin[...].astype(F32) + win[2].astype(F32) + win[3].astype(F32)
    for copy in copies:
        copy.wait_send()
    return result


def spread_out(mine, everyone, base, ssem, rsem, use):
    c, me, zp, up, down = tp_places()
    opp = lax.rem(me + 4, 8)

    def other(k):
        return k + 1 - 2 * lax.rem(k, 2)

    half = everyone.shape[1] // 2
    lo, hi = pl.ds(0, half), pl.ds(half, half)
    copies = []

    def cp(k, slot, to, part=None):
        ref = everyone.at[slot] if part is None else everyone.at[slot, part]
        copy = remote(ref, ref, ssem.at[base + k], rsem.at[base + k], (c, to))
        copy.start()
        copies.append(copy)
        return copy

    everyone[me] = mine
    c1 = [cp(0, me, up, lo)]
    c2 = [cp(1, me, down, hi)]
    c0 = [cp(2, me, zp, lo)]
    c1.append(cp(3, me, up, hi))
    c2.append(cp(4, me, down, lo))
    c0.append(cp(5, me, zp, hi))
    use(me)
    c1[0].wait_recv()
    c5 = cp(6, down, up, lo)
    c2[0].wait_recv()
    c6 = cp(7, up, down, hi)
    c0[0].wait_recv()
    late = [cp(8, zp, up, lo), cp(9, zp, down, lo)]
    c0[1].wait_recv()
    late += [cp(10, zp, up, hi), cp(11, zp, down, hi)]
    use(zp)
    c5.wait_recv()
    c7 = cp(12, opp, zp, lo)
    c1[1].wait_recv()
    use(down)
    c6.wait_recv()
    c8 = cp(13, opp, zp, hi)
    c2[1].wait_recv()
    use(up)
    use(opp)
    for copy in late:
        copy.wait_recv()
    use(other(down))
    use(other(up))
    c7.wait_recv()
    c8.wait_recv()
    use(other(opp))
    for copy in copies:
        copy.wait_send()


def prefix_weights(logs, heads):
    tp, me, core, x, zh, at = ctx_places()
    j = lax.broadcasted_iota(jnp.int32, (16, 128), 0)
    jz, jx, jc = j // 8, lax.rem(j // 2, 4), lax.rem(j, 2)

    def factor(mask, scale):
        log = dot(logs, jnp.where(mask, 1.0, 0.0), (0, 0), HIGH)
        return jnp.exp(log) * scale

    one = jnp.float32(1.0)
    zero = jnp.float32(0.0)
    same = (jz == zh) & (jx == x)
    rows = [
        factor(same & (jc + 1 == core), one),
        factor(same & (jc + core == 0), one),
    ]
    for d in range(4):
        rows.append(factor((jz == zh) & (jx < lax.rem(x + d, 4)), one))
    for d in range(4):
        to = lax.rem(x + d, 4)
        rows.append(
            factor((jz == zh) & (jx > x) & (jx < to), jnp.where(to > x, one, zero))
        )
    rows.append(factor((jz == 0) & (jx > x), jnp.where(zh == 0, one, zero)))
    rows.append(factor(same & (jc == core + 1), one))
    rows.append(jnp.full((heads, 128), jnp.where(core == 0, one, zero)))
    return rows


def whole_kernel(
    kv_hbm, q_hbm, g_hbm, hid_hbm, qw_hbm, kw_hbm, ow_hbm, mw_hbm, up_hbm, b_hbm, c_hbm,
    step_ref, decay_ref, seg_ref, skip_ref,
    mid_ref, hidden_ref, state_ref,
    kv, kvall, s_ref, q4, g4, top, t4, d4, p,
    got, uin, vin, zin, tout, uout, zout, dq_ref, kvg_ref, hid, cum_ref, cumt_ref, steps, logs,
    qw, kw, ow, mw, up_ref, b_ref, c_ref, tin, tuin, rin, rv, rout, everyone, y_acc, y, mixed,
    local, w_ref, terms, ours_out, theirs, gx, hout, hin, eout, ein, carried,
    ssem, rsem, hssem, hrsem, tssem, trsem, lsem,
):
    tp, me, core, x, zh, at = ctx_places()
    c, tme, tzp, tup, tdown = tp_places()
    topp = lax.rem(tme + 4, 8)
    mate = at(zh, x, 1 - core)
    right, left, opp = at(zh, x + 1, core), at(zh, x + 3, core), at(zh, x + 2, core)
    zp = at(1 - zh, x, core)
    heads, rows, size = q4.shape
    scaling = size ** (-0.5)
    own_rows = pl.ds(0, rows)
    loads = [pltpu.make_async_copy(kv_hbm, kv.at[own_rows], lsem.at[0])]
    hid_own = pltpu.make_async_copy(hid_hbm, hid.at[tme], lsem.at[1])
    weights = [
        pltpu.make_async_copy(src, dst, lsem.at[2 + k])
        for k, (src, dst) in enumerate(((qw_hbm, qw), (kw_hbm, kw), (ow_hbm, ow), (mw_hbm, mw)))
    ]
    more = [
        pltpu.make_async_copy(src, dst, lsem.at[6 + k])
        for k, (src, dst) in enumerate(((up_hbm, up_ref), (b_hbm, b_ref), (c_hbm, c_ref)))
    ]
    for h in range(heads):
        lanes = pl.ds(h * size, size)
        loads.append(pltpu.make_async_copy(q_hbm.at[:, lanes], q4.at[h], lsem.at[9 + h]))
        loads.append(pltpu.make_async_copy(g_hbm.at[:, lanes], g4.at[h], lsem.at[9 + heads + h]))
    loads[0].start()
    hid_own.start()
    for load in loads[1:] + weights + more:
        load.start()
    barrier = pltpu.get_barrier_semaphore()
    peers = [(c, tzp), (c, tup), (c, tdown), (mate, tp), (right, tp), (left, tp), (zp, tp)]
    for peer in peers:
        pl.semaphore_signal(barrier, inc=1, device_id=peer, device_id_type=MESH)

    groups = step_ref.shape[0]
    tri = lower(rows)
    eye = jnp.where(
        lax.broadcasted_iota(jnp.int32, (groups, groups), 0)
        == lax.broadcasted_iota(jnp.int32, (groups, groups), 1),
        -decay_ref[...],
        0.0,
    )
    log_step = dot(eye, step_ref[...], (1, 0), HIGH)
    cum_ref[...] = dot(tri, log_step, (1, 1), HIGH)
    cumt_ref[...] = dot(log_step, tri, (1, 1), HIGH)
    row = lax.broadcasted_iota(jnp.int32, (rows, rows), 0)
    col = lax.broadcasted_iota(jnp.int32, (rows, rows), 1)
    steps[...] = dot(jnp.where(row == col, 1.0, 0.0), step_ref[...], (1, 1), HIGH)
    pad = jnp.zeros((16, 2 * size - groups), F32)
    total = jnp.concatenate(
        [jnp.broadcast_to(cum_ref[pl.ds(rows - 1, 1)], (16, groups)), pad], axis=1
    )
    line = lax.broadcasted_iota(jnp.int32, total.shape, 0)
    one = total.astype(BF16).astype(F32)
    two = (total - one).astype(BF16).astype(F32)
    kv[pl.ds(rows, 16)] = jnp.where(
        line == 0, one, jnp.where(line == 1, two, jnp.where(line == 2, total - one - two, 0.0))
    ).astype(BF16)
    seg = jnp.where(seg_ref[...] == 0, 1.0, 0.0)
    bound = jnp.sum(jnp.sum(seg, axis=1, keepdims=True), axis=0, keepdims=True)
    loads[0].wait()
    pl.semaphore_wait(barrier, len(peers))

    sent = []

    def cp(k, slot, to, part=None, own=False):
        dst = kvall.at[slot] if part is None else kvall.at[slot, part]
        from_kv = kv if part is None else kv.at[part]
        copy = remote(from_kv if own else dst, dst, ssem.at[k], rsem.at[k], (to, tp))
        copy.start()
        sent.append(copy)
        return copy

    def hp(k, slot, to, part=None):
        dst = hid.at[slot] if part is None else hid.at[slot, part]
        copy = remote(dst, dst, hssem.at[k], hrsem.at[k], (c, to))
        copy.start()
        sent.append(copy)
        return copy

    lo, hi = pl.ds(0, 128), pl.ds(128, kv.shape[0] - 128)
    z0 = [cp(0, me, zp, lo, own=True)]
    r0 = [cp(1, me, right, lo, own=True)]
    l0 = [cp(2, me, left, hi, own=True)]
    z0.append(cp(3, me, zp, hi, own=True))
    r0.append(cp(4, me, right, hi, own=True))
    l0.append(cp(5, me, left, lo, own=True))
    m0 = cp(6, me, mate, own=True)
    mine = pltpu.make_async_copy(kv, kvall.at[me], lsem.at[0])
    mine.start()
    hid_own.wait()
    h1 = hp(1, tme, tup)
    h2 = hp(2, tme, tdown)

    y_acc[:, : heads * size] = jnp.full((rows, heads * size), -jnp.inf, F32)
    local[...] = jnp.zeros_like(local)
    y_acc[:, heads * size :] = jnp.zeros((rows, heads * size), F32)
    p[...] = jnp.zeros_like(p)
    reach = 3 * 4096 // (4 * rows)
    first = jnp.maximum(me - reach, 0)
    for load in loads[1:]:
        load.wait()
    q_pos = (me * rows + row).astype(F32)
    floor = jnp.where(q_pos >= bound, bound, 0.0)

    def twice(a):
        return jnp.concatenate([a, a], axis=1)

    def scores(j):
        @pl.when((j <= me) & (j >= first))
        def _():
            k = kvall[j, :rows, :size]
            k_pos = (j * rows + col).astype(F32)
            bias = jnp.where((k_pos <= q_pos) & (k_pos >= floor), 0.0, -1e30)
            for h in range(heads):
                s = dot(q4[h], k, (1, 1)) + bias
                s_ref[j - first, h] = s
                y_acc[:, h * size : (h + 1) * size] = jnp.maximum(y_acc[:, h * size : (h + 1) * size], jnp.maximum(s[:, :size], s[:, size:]))

    def weigh(low, high, use_it, group):
        def step(j, _):
            @pl.when(use_it(j) & (j <= me) & (j >= first))
            def _():
                v = jnp.concatenate([kvall[j, :rows, size:], jnp.ones((rows, size), BF16)], axis=1)
                for h in range(heads):
                    e = jnp.exp((s_ref[j - first, h] - twice(top[group, h])) * scaling)
                    s_ref[j - first, h] = e
                    local[:, 2 * h * size : (2 * h + 2) * size] += dot(e.astype(BF16), v, (1, 0))

            return 0

        lax.fori_loop(low, high, step, 0)

    def raise_top(group):
        for h in range(heads):
            high = jnp.broadcast_to(jnp.max(y_acc[:, h * size : (h + 1) * size], axis=1, keepdims=True), (rows, size))
            if group > 0:
                local[:, 2 * h * size : (2 * h + 2) * size] = local[:, 2 * h * size : (2 * h + 2) * size] * twice(jnp.exp((top[group - 1, h] - high) * scaling))
            top[group, h] = high

    def always(j):
        return j >= 0

    mine.wait()
    scores(me)
    r0[0].wait_recv()
    f1 = cp(7, left, right, lo)
    l0[0].wait_recv()
    f2 = cp(8, right, left, hi)
    m0.wait_recv()
    scores(mate)
    z0[0].wait_recv()
    zr = [cp(9, zp, right, lo)]
    zl = [cp(10, zp, left, lo)]
    r0[1].wait_recv()
    m1 = cp(11, left, mate)
    l0[1].wait_recv()
    m2 = cp(12, right, mate)
    z0[1].wait_recv()
    zl.append(cp(13, zp, left, hi))
    zr.append(cp(14, zp, right, hi))
    m3 = cp(15, zp, mate)
    h0 = hp(0, tme, tzp)
    scores(left)
    f1.wait_recv()
    m4 = cp(16, opp, mate, lo)
    f2.wait_recv()
    m5 = cp(17, opp, mate, hi)
    scores(right)
    scores(opp)
    m1.wait_recv()
    scores(at(zh, x + 3, 1 - core))
    zright, zleft, zopp = at(1 - zh, x + 1, core), at(1 - zh, x + 3, core), at(1 - zh, x + 2, core)
    zr[0].wait_recv()
    f3 = cp(18, zleft, right, lo)
    m2.wait_recv()
    scores(at(zh, x + 1, 1 - core))
    m4.wait_recv()
    m5.wait_recv()
    scores(at(zh, x + 2, 1 - core))
    raise_top(0)
    zl[1].wait_recv()
    f4 = cp(19, zright, left, hi)
    zr[1].wait_recv()
    m6 = cp(20, zleft, mate)
    zl[0].wait_recv()
    m7 = cp(21, zright, mate)
    near_low = jnp.maximum(first, zh * 8)
    near_mid = (near_low + me + 1) // 2
    weigh(near_low, near_mid, always, 0)
    f3.wait_recv()
    m8 = cp(22, zopp, mate, lo)
    f4.wait_recv()
    m9 = cp(23, zopp, mate, hi)
    weigh(near_mid, me + 1, always, 0)
    h0.wait_recv()
    h1.wait_recv()
    h2.wait_recv()
    h5 = hp(5, tdown, tup, pl.ds(0, 128))
    h6 = hp(6, tup, tdown, pl.ds(128, 128))
    h3 = hp(3, tzp, tup)
    h4 = hp(4, tzp, tdown)
    scores(zp)
    scores(zleft)
    scores(zright)
    m3.wait_recv()
    scores(at(1 - zh, x, 1 - core))
    m6.wait_recv()
    scores(at(1 - zh, x + 3, 1 - core))
    m7.wait_recv()
    scores(at(1 - zh, x + 1, 1 - core))
    raise_top(1)
    far = lax.rem(x + 2, 4)
    away = (1 - zh) * 8
    weigh(away, away + 8, lambda j: lax.rem(j // 2, 4) != far, 1)
    scores(zopp)
    m8.wait_recv()
    m9.wait_recv()
    scores(at(1 - zh, x + 2, 1 - core))
    raise_top(2)
    weigh(away + 2 * far, away + 2 * far + 2, always, 2)

    logs[...] = (
        kvall[:, rows, :groups].astype(F32)
        + kvall[:, rows + 1, :groups].astype(F32)
        + kvall[:, rows + 2, :groups].astype(F32)
    )
    for h in range(heads):
        inverse = 1.0 / local[:, (2 * h + 1) * size : (2 * h + 2) * size]
        out = local[:, 2 * h * size : (2 * h + 1) * size] * inverse
        corr = jnp.sum(out * g4[h].astype(F32), axis=1, keepdims=True)
        y_acc[:, h * size : (h + 1) * size] = jnp.broadcast_to(corr, (rows, size))
        last = top[2, h]
        for group in range(3):
            top[group, h] = inverse * jnp.exp((top[group, h] - last) * scaling)

    h5.wait_recv()
    h7 = hp(7, topp, tzp, pl.ds(0, 128))
    h6.wait_recv()
    h8 = hp(8, topp, tzp, pl.ds(128, 128))

    def grads(d, c_at):
        def one_z(n, _):
            z = jnp.where(n == 0, 1 - zh, zh)
            group = jnp.where(n == 0, 2 if d == 2 else 1, 0)
            j = at(z, x + d, c_at)

            @pl.when((j <= me) & (j >= first))
            def _():
                k = kvall[j, :rows, :size]
                v = kvall[j, :rows, size:]
                for h in range(heads):
                    t = s_ref[j - first, h] * twice(top[group, h])
                    e = (t * (dot(g4[h], v, (1, 1)) - twice(y_acc[:, h * size : (h + 1) * size]))).astype(BF16)
                    t4[h] = t.astype(BF16)
                    d4[h] = e
                    y_acc[:, (heads + h) * size : (heads + h + 1) * size] += dot(e, k, (1, 0))
                dk = dot(d4[...].reshape(heads * rows, rows), q4[...].reshape(heads * rows, size), (0, 0))
                dv = dot(t4[...].reshape(heads * rows, rows), g4[...].reshape(heads * rows, size), (0, 0))
                p[z, lax.rem(x + d, 4), c_at] = jnp.concatenate([dk * scaling, dv], axis=1).astype(BF16)

            return 0

        lax.fori_loop(0, 2, one_z, 0)

    half = rows // 2
    low, high = pl.ds(0, half), pl.ds(half, half)

    def sp(k, src, dst, to):
        copy = remote(src, dst, ssem.at[24 + k], rsem.at[24 + k], (to, tp))
        copy.start()
        sent.append(copy)
        return copy

    def to_mate(k, d):
        grads(d, 1 - core)
        return sp(k, p.at[:, lax.rem(x + d, 4), 1 - core], got.at[d], mate)

    def both(d, z):
        return p[z, lax.rem(x + d, 4), core].astype(F32) + got[d, z].astype(F32)

    order = (1 - zh, zh)
    g2 = to_mate(0, 2)
    grads(2, core)
    g2.wait_recv()
    t0, t1, u0, u1 = [], [], [], []
    for n, z in enumerate(order):
        tout[z] = both(2, z).astype(BF16)
        t0.append(sp(4 + n, tout.at[z, low], uin.at[0, z], right))
        t1.append(sp(6 + n, tout.at[z, high], uin.at[1, z], left))
    g1 = to_mate(1, 1)
    grads(1, core)
    g3 = to_mate(2, 3)
    grads(3, core)
    g1.wait_recv()
    g3.wait_recv()
    for n, z in enumerate(order):
        u = both(1, z)
        uout[0, z, high] = u[half:].astype(BF16)
        t0[n].wait_recv()
        uout[0, z, low] = (u[:half] + uin[0, z].astype(F32)).astype(BF16)
        u0.append(sp(8 + n, uout.at[0, z], vin.at[0, z], right))
        u = both(3, z)
        uout[1, z, low] = u[:half].astype(BF16)
        t1[n].wait_recv()
        uout[1, z, high] = (u[half:] + uin[1, z].astype(F32)).astype(BF16)
        u1.append(sp(10 + n, uout.at[1, z], vin.at[1, z], left))
    g0 = to_mate(3, 0)
    grads(0, core)
    for h in range(heads):
        dq_ref[:, h * size : (h + 1) * size] = (y_acc[:, (heads + h) * size : (heads + h + 1) * size] * scaling).astype(BF16)
    g0.wait_recv()

    def whole(n, z):
        u0[n].wait_recv()
        u1[n].wait_recv()
        return (
            p[z, x, core].astype(F32)
            + got[0, z].astype(F32)
            + vin[0, z].astype(F32)
            + vin[1, z].astype(F32)
        )

    zout[...] = whole(0, 1 - zh).astype(BF16)
    zc = sp(12, zout, zin, zp)
    kept = whole(1, zh)
    zc.wait_recv()
    kvg_ref[...] = (kept + zin[...].astype(F32)).astype(BF16)
    h3.wait_recv()
    h4.wait_recv()
    h7.wait_recv()
    h8.wait_recv()
    for copy in sent:
        copy.wait_send()

    width = up_ref.shape[1]
    inner = mixed.shape[1]
    state_size = inner // groups

    def part(k):
        return pl.ds(pl.multiple_of(k * width, width), width)

    for index, value in enumerate(prefix_weights(logs[...], groups)):
        w_ref[index] = value
    weights[0].wait()
    weights[1].wait()
    for load in more:
        load.wait()

    def attn_term(k):
        return dot(dq_ref[...], qw[part(k)], (1, 1)) + dot(kvg_ref[...], kw[part(k)], (1, 1))

    def mix():
        weights[3].wait()

        def step(k, _):
            y_acc[...] += dot(hid[k], mw[part(k)], (1, 0))
            return 0

        y_acc[...] = jnp.zeros_like(y_acc)
        lax.fori_loop(0, 8, step, 0)
        mixed[...] = y_acc[...].astype(BF16)

    mid = sent_sums(
        attn_term, lambda: up_ref[...].astype(F32), (tin, tuin, rin, rv, rout), 0, tssem, trsem, mix
    ).astype(BF16)
    mid_ref[...] = mid
    weights[2].wait()
    y_acc[...] = jnp.zeros_like(y_acc)

    def out_term(k):
        y_acc[...] += dot(everyone[k], ow[:, part(k)], (1, 1))

    spread_out(mid, everyone, 14, tssem, trsem, out_term)
    y[...] = y_acc[...].astype(BF16)

    spot = lax.broadcasted_iota(jnp.int32, (groups, inner), 1)
    head = lax.broadcasted_iota(jnp.int32, (groups, inner), 0) * state_size
    wide = jnp.where((spot >= head) & (spot < head + state_size), 1.0, 0.0).astype(BF16)

    def widen(value):
        high = value.astype(BF16)
        low = (value - high.astype(F32)).astype(BF16)
        return dot(high, wide, (1, 0)) + dot(low, wide, (1, 0))

    cum = cum_ref[...]
    weighted = (y[...].astype(F32) * widen(jnp.exp(cum))).astype(BF16)
    terms[...] = dot(weighted, c_ref[...], (0, 0)).reshape(terms.shape)
    count = groups // 2
    begin = core * count
    half = count // 2
    theirs_at = pl.ds((1 - core) * count, count)
    ours = pl.ds(begin, count)
    copies = []

    def pp(k, src, dst, to):
        copy = remote(src, dst, tssem.at[28 + k], trsem.at[28 + k], (to, tp))
        copy.start()
        copies.append(copy)
        return copy

    ours_out[...] = terms[...].astype(BF16)
    a_heads, b_heads = pl.ds(0, half), pl.ds(half, half)
    away_at = (1 - core) * count
    c0 = [
        pp(n, ours_out.at[pl.ds(away_at + n * half, half)], theirs.at[pl.ds(away_at + n * half, half)], mate)
        for n in range(2)
    ]
    c1 = pp(2, ours_out.at[ours], theirs.at[ours], mate)

    def w(k, h):
        return w_ref[k, pl.ds(begin + h, 1), :]

    inner_bc = dot(b_ref[...], c_ref[...], (1, 1))
    later = col >= row
    left_lane = lax.broadcasted_iota(jnp.int32, (rows, 2 * state_size), 1) < state_size

    def decay(h):
        spread = cumt_ref[pl.ds(h, 1), :] - cum_ref[:, h : h + 1]
        return jnp.exp(jnp.where(later, spread, -1e30))

    def pair_of(ref, p):
        both = ref[:, p * 2 * state_size : (p + 1) * 2 * state_size]
        none = jnp.zeros_like(both)
        return jnp.where(left_lane, both, none), jnp.where(left_lane, none, both), both

    def local_pairs(start, stop):
        for p in range(start, stop):
            y0, y1, _ = pair_of(y, p)
            a0 = (inner_bc * decay(2 * p)).astype(BF16)
            a1 = (inner_bc * decay(2 * p + 1)).astype(BF16)
            local[:, p * 2 * state_size : (p + 1) * 2 * state_size] = dot(a0, y0, (1, 0)) + dot(a1, y1, (1, 0))

    def chip_terms(n):
        c0[n].wait_recv()
        for h in range(n * half, (n + 1) * half):
            gx[0, h] = (
                w(0, h) * terms[begin + h] + w(1, h) * theirs[begin + h].astype(F32)
            ).astype(BF16)

    chip_terms(0)
    r0a = pp(3, gx.at[0, a_heads], gx.at[3, a_heads], right)
    chip_terms(1)
    l0b = pp(4, gx.at[0, b_heads], gx.at[1, b_heads], left)
    l0a = pp(5, gx.at[0, a_heads], gx.at[1, a_heads], left)
    r0b = pp(6, gx.at[0, b_heads], gx.at[3, b_heads], right)
    local_pairs(0, 2)
    r0a.wait_recv()
    r1 = pp(7, gx.at[3, a_heads], gx.at[2, a_heads], right)
    l0b.wait_recv()
    l1 = pp(8, gx.at[1, b_heads], gx.at[2, b_heads], left)
    local_pairs(2, 5)

    def weigh_states(base, h):
        return sum(w(base + d, h) * gx[d, h].astype(F32) for d in range(4))

    l0a.wait_recv()
    r1.wait_recv()
    for h in range(half):
        hout[h] = weigh_states(2, h).astype(BF16)
    z0a = pp(9, hout.at[a_heads], hin.at[a_heads], zp)
    r0b.wait_recv()
    l1.wait_recv()
    for h in range(half, count):
        hout[h] = weigh_states(2, h).astype(BF16)
    z0b = pp(10, hout.at[b_heads], hin.at[b_heads], zp)
    local_pairs(5, 8)
    e0 = []
    for n, (z_n, part_n) in enumerate(((z0a, a_heads), (z0b, b_heads))):
        z_n.wait_recv()
        for h in range(n * half, (n + 1) * half):
            eout[h] = (weigh_states(6, h) + w(10, h) * hin[h].astype(F32)).astype(BF16)
        e0.append(pp(11 + n, eout.at[part_n], ein.at[part_n], mate))
    c1.wait_recv()

    def finish(start, e):
        for h in range(count):
            at_h = pl.ds(start + h, 1)
            carried[start + h] = (
                w_ref[12, at_h, :] * theirs[start + h].astype(F32)
                + w_ref[11, at_h, :] * e[h].astype(F32)
            ).astype(BF16)

    finish(begin, eout)
    ending = widen(jnp.exp(cum_ref[pl.ds(rows - 1, 1)] - cum))
    stepping = widen(steps[...])
    skipping = widen(jnp.broadcast_to(skip_ref[...], (rows, groups)))
    for copy in e0:
        copy.wait_recv()
    finish((1 - core) * count, ein)
    state = carried[...].reshape(inner, terms.shape[2])
    y_float = y[...].astype(F32)
    grad_in = (
        stepping * (local[...] + dot(b_ref[...], state, (1, 1)) * ending) + skipping * y_float
    ).astype(BF16)
    y_acc[...] = stepping * ending

    def mix_term(k):
        return dot(grad_in, mw[part(k)], (1, 1))

    def states():
        scaled = (mixed[...].astype(F32) * y_acc[...]).astype(BF16)
        s_ref[0, 0] = jnp.zeros((rows, rows), F32)
        for p in range(groups // 2):
            m0, m1, _ = pair_of(mixed, p)
            both = y[:, p * 2 * state_size : (p + 1) * 2 * state_size]
            for h, m in ((2 * p, m0), (2 * p + 1, m1)):
                s_ref[0, 0] += dot(m, both, (1, 1)) * decay(h) * steps[:, h : h + 1]
        state_ref[...] = dot(s_ref[0, 0].astype(BF16), c_ref[...], (1, 0)) + dot(
            scaled, state, (1, 0)
        )

    hidden_ref[...] = sent_sums(
        mix_term, lambda: mid_ref[...].astype(F32), (tin, tuin, rin, rv, rout), 42, tssem, trsem, states
    ).astype(BF16)
    for copy in copies:
        copy.wait_send()


def whole(arrays, cid):
    keyval, query, _, hidden, qw, kw, ow, mw, upstream, b, c, step = arrays[:12]
    rows, cols = keyval.shape
    size = cols // 2
    heads = query.shape[1] // size
    groups = step.shape[0]
    inner = mw.shape[1]
    full = upstream.shape
    state = (groups, inner // groups, b.shape[1])
    part = (groups // 2,) + state[1:]
    any_spec = pl.BlockSpec(memory_space=pl.ANY)
    two = (2, rows, cols)
    vm = pltpu.VMEM
    dma = pltpu.SemaphoreType.DMA
    return pl.pallas_call(
        whole_kernel,
        out_shape=(
            jax.ShapeDtypeStruct(full, BF16),
            jax.ShapeDtypeStruct(full, BF16),
            jax.ShapeDtypeStruct((rows, b.shape[1]), F32),
        ),
        in_specs=[any_spec] * 11 + [VM] * 4,
        out_specs=(VM,) * 3,
        scratch_shapes=[
            vm((rows + 16, cols), BF16),
            vm((16, rows + 16, cols), BF16),
            vm((13, heads, rows, rows), F32),
            vm((heads, rows, size), BF16),
            vm((heads, rows, size), BF16),
            vm((3, heads, rows, size), F32),
            vm((heads, rows, rows), BF16),
            vm((heads, rows, rows), BF16),
            vm((2, 4, 2, rows, cols), BF16),
            vm((4,) + two, BF16),
            vm((2, 2, rows // 2, cols), BF16),
            vm((2,) + two, BF16),
            vm((rows, cols), BF16),
            vm(two, BF16),
            vm((2,) + two, BF16),
            vm((rows, cols), BF16),
            vm(query.shape, BF16),
            vm(keyval.shape, BF16),
            vm((8,) + hidden.shape, BF16),
            vm((rows, groups), F32),
            vm((groups, rows), F32),
            vm((rows, groups), F32),
            vm((16, groups), F32),
            vm(qw.shape, BF16),
            vm(kw.shape, BF16),
            vm(ow.shape, BF16),
            vm(mw.shape, BF16),
            vm(full, BF16),
            vm(b.shape, BF16),
            vm(c.shape, BF16),
            vm(full, BF16),
            vm((2, rows // 2, full[1]), BF16),
            vm((4,) + full, BF16),
            vm(full, BF16),
            vm((7,) + full, BF16),
            vm((8,) + full, BF16),
            vm((rows, inner), F32),
            vm((rows, inner), BF16),
            vm((rows, inner), BF16),
            vm((rows, inner), F32),
            vm((13, groups, 128), F32),
            vm(state, F32),
            vm(state, BF16),
            vm(state, BF16),
            vm((4,) + part, BF16),
            vm(part, BF16),
            vm(part, BF16),
            vm(part, BF16),
            vm(part, BF16),
            vm(state, BF16),
            dma((37,)),
            dma((37,)),
            dma((9,)),
            dma((9,)),
            dma((56,)),
            dma((56,)),
            dma((17,)),
        ],
        compiler_params=pltpu.CompilerParams(
            collective_id=cid, has_side_effects=True, vmem_limit_bytes=(64 << 20) - (256 << 10)
        ),
        name="whole",
    )(*arrays)


def finish_kernel(a_ref, b_ref, c_ref, a_out, b_out, c_out):
    a_out[...] = a_ref[...]
    b_out[...] = b_ref[...]
    c_out[...] = c_ref[...]


def finish(arrays):
    return pl.pallas_call(
        finish_kernel,
        out_shape=tuple(jax.ShapeDtypeStruct(a.shape, a.dtype) for a in arrays),
        in_specs=[VM] * 3,
        out_specs=(VM,) * 3,
        name="finish",
    )(*arrays)


def on_device(
    hidden_in,
    upstream,
    query_ckpt,
    keyval_ckpt,
    attn_out_grad,
    segments,
    query_weight,
    keyval_weight,
    mix_weight,
    out_weight,
    state_in_ckpt,
    state_out_ckpt,
    step_size,
    decay_rate,
    skip_gain,
):
    return finish(
        whole(
            (
                keyval_ckpt,
                query_ckpt,
                attn_out_grad,
                hidden_in,
                query_weight,
                keyval_weight,
                out_weight,
                mix_weight,
                upstream,
                state_in_ckpt,
                state_out_ckpt,
                step_size.T,
                decay_rate[None, :],
                segments.reshape(-1, 128),
                skip_gain[None, :],
            ),
            1,
        )
    )


def solution(mesh):
    placed = (
        P("ctx", "tp"),
        P("ctx", "tp"),
        P("ctx", "tp"),
        P("ctx", "tp"),
        P("ctx", "tp"),
        P(),
        P(None, "tp"),
        P(None, "tp"),
        P(None, "tp"),
        P("tp", None),
        P("ctx", "tp"),
        P("ctx", "tp"),
        P("ctx", "tp"),
        P("tp"),
        P("tp"),
    )
    return jax.shard_map(
        on_device,
        mesh=mesh,
        in_specs=placed,
        out_specs=(P("ctx", "tp"), P("ctx", "tp"), P("ctx", "tp")),
        check_vma=False,
    )
```

```python
import jax
import jax.numpy as jnp
from jax import lax
from jax.experimental import pallas as pl
from jax.experimental.pallas import tpu as pltpu
from jax.sharding import PartitionSpec as P

HIGH = lax.Precision.HIGHEST
MESH = pl.DeviceIdType.MESH
VM = pl.BlockSpec(memory_space=pltpu.VMEM)
F32 = jnp.float32
BF16 = jnp.bfloat16


def remote(src, dst, send, recv, to):
    return pltpu.make_async_remote_copy(
        src_ref=src, dst_ref=dst, send_sem=send, recv_sem=recv, device_id=to, device_id_type=MESH
    )


def greet(peers):
    barrier = pltpu.get_barrier_semaphore()
    for peer in peers:
        pl.semaphore_signal(barrier, inc=1, device_id=peer, device_id_type=MESH)
    pl.semaphore_wait(barrier, len(peers))


def params(cid, mib=40):
    return pltpu.CompilerParams(
        collective_id=cid, has_side_effects=True, vmem_limit_bytes=mib << 20
    )


def tp_places():
    c = lax.axis_index("ctx")
    me = lax.axis_index("tp")
    zp = me + 1 - 2 * lax.rem(me, 2)
    return c, me, zp, lax.rem(me + 2, 8), lax.rem(me + 6, 8)


def ctx_places():
    tp = lax.axis_index("tp")
    me = lax.axis_index("ctx")
    core = lax.rem(me, 2)
    x = lax.rem(me // 2, 4)
    zh = me // 8

    def at(z, place, c):
        return z * 8 + lax.rem(place, 4) * 2 + c

    return tp, me, core, x, zh, at


def dot(left, right, over, precision=None):
    return lax.dot_general(
        left,
        right,
        (((over[0],), (over[1],)), ((), ())),
        preferred_element_type=F32,
        precision=precision,
    )


def lower(n):
    row = lax.broadcasted_iota(jnp.int32, (n, n), 0)
    col = lax.broadcasted_iota(jnp.int32, (n, n), 1)
    return (col <= row).astype(F32)


def sent_sums(term, add, buf, base, ssem, rsem, beside):
    c, me, zp, up, down = tp_places()
    opp = lax.rem(me + 4, 8)

    def other(k):
        return k + 1 - 2 * lax.rem(k, 2)

    tin, uin, win, vin, out = buf
    half = tin.shape[0] // 2
    lo, hi = pl.ds(0, half), pl.ds(half, half)
    copies = []

    def cp(k, src, dst, to):
        copy = remote(src, dst, ssem.at[base + k], rsem.at[base + k], (c, to))
        copy.start()
        copies.append(copy)
        return copy

    out[0] = term(other(opp)).astype(BF16)
    a = [cp(n, out.at[0, part], tin.at[part], zp) for n, part in enumerate((lo, hi))]
    out[1] = term(other(up)).astype(BF16)
    w0 = [cp(2, out.at[1, lo], win.at[0, lo], up)]
    out[2] = term(other(down)).astype(BF16)
    w1 = [cp(3, out.at[2, lo], win.at[1, lo], down)]
    w0.append(cp(4, out.at[1, hi], win.at[0, hi], up))
    w1.append(cp(5, out.at[2, hi], win.at[1, hi], down))
    to_up = term(up)
    out[5, hi] = to_up[half:].astype(BF16)
    to_down = term(down)
    out[6, lo] = to_down[:half].astype(BF16)
    held = term(opp)
    a[0].wait_recv()
    out[3, lo] = (held[:half] + tin[lo].astype(F32)).astype(BF16)
    t0 = cp(6, out.at[3, lo], uin.at[0], up)
    u0 = [cp(8, out.at[5, hi], win.at[2, hi], up)]
    u1 = [cp(9, out.at[6, lo], win.at[3, lo], down)]
    a[1].wait_recv()
    out[3, hi] = (held[half:] + tin[hi].astype(F32)).astype(BF16)
    t1 = cp(7, out.at[3, hi], uin.at[1], down)
    held = term(zp)
    v = []
    for n, part in enumerate((lo, hi)):
        w0[n].wait_recv()
        w1[n].wait_recv()
        rows = slice(n * half, (n + 1) * half)
        out[4, part] = (
            held[rows] + win[0, part].astype(F32) + win[1, part].astype(F32)
        ).astype(BF16)
        v.append(cp(10 + n, out.at[4, part], vin.at[part], zp))
    t0.wait_recv()
    out[5, lo] = (to_up[:half] + uin[0].astype(F32)).astype(BF16)
    u0.append(cp(12, out.at[5, lo], win.at[2, lo], up))
    t1.wait_recv()
    out[6, hi] = (to_down[half:] + uin[1].astype(F32)).astype(BF16)
    u1.append(cp(13, out.at[6, hi], win.at[3, hi], down))
    held = term(me) + add()
    beside()
    for copy in v + u0 + u1:
        copy.wait_recv()
    result = held + vin[...].astype(F32) + win[2].astype(F32) + win[3].astype(F32)
    for copy in copies:
        copy.wait_send()
    return result


def spread_out(mine, everyone, base, ssem, rsem, use):
    c, me, zp, up, down = tp_places()
    opp = lax.rem(me + 4, 8)

    def other(k):
        return k + 1 - 2 * lax.rem(k, 2)

    half = everyone.shape[1] // 2
    lo, hi = pl.ds(0, half), pl.ds(half, half)
    copies = []

    def cp(k, slot, to, part=None):
        ref = everyone.at[slot] if part is None else everyone.at[slot, part]
        copy = remote(ref, ref, ssem.at[base + k], rsem.at[base + k], (c, to))
        copy.start()
        copies.append(copy)
        return copy

    everyone[me] = mine
    c1 = [cp(0, me, up, lo)]
    c2 = [cp(1, me, down, hi)]
    c0 = [cp(2, me, zp, lo)]
    c1.append(cp(3, me, up, hi))
    c2.append(cp(4, me, down, lo))
    c0.append(cp(5, me, zp, hi))
    use(me)
    c1[0].wait_recv()
    c5 = cp(6, down, up, lo)
    c2[0].wait_recv()
    c6 = cp(7, up, down, hi)
    c0[0].wait_recv()
    late = [cp(8, zp, up, lo), cp(9, zp, down, lo)]
    c0[1].wait_recv()
    late += [cp(10, zp, up, hi), cp(11, zp, down, hi)]
    use(zp)
    c5.wait_recv()
    c7 = cp(12, opp, zp, lo)
    c1[1].wait_recv()
    use(down)
    c6.wait_recv()
    c8 = cp(13, opp, zp, hi)
    c2[1].wait_recv()
    use(up)
    use(opp)
    for copy in late:
        copy.wait_recv()
    use(other(down))
    use(other(up))
    c7.wait_recv()
    c8.wait_recv()
    use(other(opp))
    for copy in copies:
        copy.wait_send()


def prefix_weights(logs, heads):
    tp, me, core, x, zh, at = ctx_places()
    j = lax.broadcasted_iota(jnp.int32, (16, 128), 0)
    jz, jx, jc = j // 8, lax.rem(j // 2, 4), lax.rem(j, 2)

    def factor(mask, scale):
        log = dot(logs, jnp.where(mask, 1.0, 0.0), (0, 0), HIGH)
        return jnp.exp(log) * scale

    one = jnp.float32(1.0)
    zero = jnp.float32(0.0)
    same = (jz == zh) & (jx == x)
    rows = [
        factor(same & (jc + 1 == core), one),
        factor(same & (jc + core == 0), one),
    ]
    for d in range(4):
        rows.append(factor((jz == zh) & (jx < lax.rem(x + d, 4)), one))
    for d in range(4):
        to = lax.rem(x + d, 4)
        rows.append(
            factor((jz == zh) & (jx > x) & (jx < to), jnp.where(to > x, one, zero))
        )
    rows.append(factor((jz == 0) & (jx > x), jnp.where(zh == 0, one, zero)))
    rows.append(factor(same & (jc == core + 1), one))
    rows.append(jnp.full((heads, 128), jnp.where(core == 0, one, zero)))
    return rows


def whole_kernel(
    kv_hbm, q_hbm, g_hbm, hid_hbm, qw_hbm, kw_hbm, ow_hbm, mw_hbm, up_hbm, b_hbm, c_hbm,
    step_ref, decay_ref, seg_ref, skip_ref,
    mid_ref, hidden_ref, state_ref,
    kv, kvall, s_ref, q4, g4, stat, top, t4, d4, p,
    got, uin, vin, zin, tout, uout, zout, dq_ref, kvg_ref, hid, cum_ref, cumt_ref, steps, logs,
    qw, kw, ow, mw, up_ref, b_ref, c_ref, tin, tuin, rin, rv, rout, everyone, y_acc, y, mixed,
    local, w_ref, terms, ours_out, theirs, gx, hout, hin, eout, ein, carried,
    ssem, rsem, hssem, hrsem, tssem, trsem, lsem,
):
    tp, me, core, x, zh, at = ctx_places()
    c, tme, tzp, tup, tdown = tp_places()
    topp = lax.rem(tme + 4, 8)
    mate = at(zh, x, 1 - core)
    right, left, opp = at(zh, x + 1, core), at(zh, x + 3, core), at(zh, x + 2, core)
    zp = at(1 - zh, x, core)
    heads, rows, size = q4.shape
    scaling = size ** (-0.5)
    own_rows = pl.ds(0, rows)
    loads = [pltpu.make_async_copy(kv_hbm, kv.at[own_rows], lsem.at[0])]
    hid_own = pltpu.make_async_copy(hid_hbm, hid.at[tme], lsem.at[1])
    weights = [
        pltpu.make_async_copy(src, dst, lsem.at[2 + k])
        for k, (src, dst) in enumerate(((qw_hbm, qw), (kw_hbm, kw), (ow_hbm, ow), (mw_hbm, mw)))
    ]
    more = [
        pltpu.make_async_copy(src, dst, lsem.at[6 + k])
        for k, (src, dst) in enumerate(((up_hbm, up_ref), (b_hbm, b_ref), (c_hbm, c_ref)))
    ]
    for h in range(heads):
        lanes = pl.ds(h * size, size)
        loads.append(pltpu.make_async_copy(q_hbm.at[:, lanes], q4.at[h], lsem.at[9 + h]))
        loads.append(pltpu.make_async_copy(g_hbm.at[:, lanes], g4.at[h], lsem.at[9 + heads + h]))
    loads[0].start()
    hid_own.start()
    for load in loads[1:] + weights + more:
        load.start()
    barrier = pltpu.get_barrier_semaphore()
    peers = [(c, tzp), (c, tup), (c, tdown), (mate, tp), (right, tp), (left, tp), (zp, tp)]
    for peer in peers:
        pl.semaphore_signal(barrier, inc=1, device_id=peer, device_id_type=MESH)

    groups = step_ref.shape[0]
    tri = lower(rows)
    eye = jnp.where(
        lax.broadcasted_iota(jnp.int32, (groups, groups), 0)
        == lax.broadcasted_iota(jnp.int32, (groups, groups), 1),
        -decay_ref[...],
        0.0,
    )
    log_step = dot(eye, step_ref[...], (1, 0), HIGH)
    cum_ref[...] = dot(tri, log_step, (1, 1), HIGH)
    cumt_ref[...] = dot(log_step, tri, (1, 1), HIGH)
    row = lax.broadcasted_iota(jnp.int32, (rows, rows), 0)
    col = lax.broadcasted_iota(jnp.int32, (rows, rows), 1)
    steps[...] = dot(jnp.where(row == col, 1.0, 0.0), step_ref[...], (1, 1), HIGH)
    pad = jnp.zeros((16, 2 * size - groups), F32)
    total = jnp.concatenate(
        [jnp.broadcast_to(cum_ref[pl.ds(rows - 1, 1)], (16, groups)), pad], axis=1
    )
    line = lax.broadcasted_iota(jnp.int32, total.shape, 0)
    one = total.astype(BF16).astype(F32)
    two = (total - one).astype(BF16).astype(F32)
    kv[pl.ds(rows, 16)] = jnp.where(
        line == 0, one, jnp.where(line == 1, two, jnp.where(line == 2, total - one - two, 0.0))
    ).astype(BF16)
    seg = jnp.where(seg_ref[...] == 0, 1.0, 0.0)
    bound = jnp.sum(jnp.sum(seg, axis=1, keepdims=True), axis=0, keepdims=True)
    loads[0].wait()
    pl.semaphore_wait(barrier, len(peers))

    sent = []

    def cp(k, slot, to, part=None, own=False):
        dst = kvall.at[slot] if part is None else kvall.at[slot, part]
        from_kv = kv if part is None else kv.at[part]
        copy = remote(from_kv if own else dst, dst, ssem.at[k], rsem.at[k], (to, tp))
        copy.start()
        sent.append(copy)
        return copy

    def hp(k, slot, to, part=None):
        dst = hid.at[slot] if part is None else hid.at[slot, part]
        copy = remote(dst, dst, hssem.at[k], hrsem.at[k], (c, to))
        copy.start()
        sent.append(copy)
        return copy

    lo, hi = pl.ds(0, 128), pl.ds(128, kv.shape[0] - 128)
    z0 = [cp(0, me, zp, lo, own=True)]
    r0 = [cp(1, me, right, lo, own=True)]
    l0 = [cp(2, me, left, hi, own=True)]
    z0.append(cp(3, me, zp, hi, own=True))
    r0.append(cp(4, me, right, hi, own=True))
    l0.append(cp(5, me, left, lo, own=True))
    m0 = cp(6, me, mate, own=True)
    mine = pltpu.make_async_copy(kv, kvall.at[me], lsem.at[0])
    mine.start()
    hid_own.wait()
    h1 = hp(1, tme, tup)
    h2 = hp(2, tme, tdown)

    stat[...] = jnp.full_like(stat, -jnp.inf)
    local[...] = jnp.zeros_like(local)
    y_acc[...] = jnp.zeros_like(y_acc)
    p[...] = jnp.zeros_like(p)
    reach = 3 * 4096 // (4 * rows)
    first = jnp.maximum(me - reach, 0)
    for load in loads[1:]:
        load.wait()
    q_pos = (me * rows + col).astype(F32)
    floor = jnp.where(q_pos >= bound, bound, 0.0)

    tall = size + 16

    def lanes_of(h):
        return slice(h * rows, (h + 1) * rows)

    def scores(j):
        @pl.when((j <= me) & (j >= first))
        def _():
            k = kvall[j, :rows, :size]
            k_pos = (j * rows + row).astype(F32)
            bias = jnp.where((k_pos <= q_pos) & (k_pos >= floor), 0.0, -1e30)
            for h in range(heads):
                s = dot(k, q4[h], (1, 1)) + bias
                s_ref[j - first, h] = s
                stat[h] = jnp.maximum(stat[h], jnp.max(s.reshape(rows // 8, 8, rows), axis=0))

    def weigh(low, high, use_it, group):
        def step(j, _):
            @pl.when(use_it(j) & (j <= me) & (j >= first))
            def _():
                v = kvall[j, :rows, size:].astype(F32).T.astype(BF16)
                v = jnp.concatenate([v, jnp.ones((16, rows), BF16)], axis=0)
                for h in range(heads):
                    e = jnp.exp((s_ref[j - first, h] - top[group, h, 0:1, :]) * scaling)
                    s_ref[j - first, h] = e
                    local[:tall, lanes_of(h)] += dot(v, e.astype(BF16), (1, 0))

            return 0

        lax.fori_loop(low, high, step, 0)

    def raise_top(group):
        for h in range(heads):
            high = jnp.max(stat[h], axis=0, keepdims=True)
            if group > 0:
                local[:tall, lanes_of(h)] = local[:tall, lanes_of(h)] * jnp.exp(
                    (top[group - 1, h, 0:1, :] - high) * scaling
                )
            top[group, h] = jnp.broadcast_to(high, (8, rows))

    def always(j):
        return j >= 0

    mine.wait()
    scores(me)
    r0[0].wait_recv()
    f1 = cp(7, left, right, lo)
    l0[0].wait_recv()
    f2 = cp(8, right, left, hi)
    m0.wait_recv()
    scores(mate)
    z0[0].wait_recv()
    zr = [cp(9, zp, right, lo)]
    zl = [cp(10, zp, left, lo)]
    r0[1].wait_recv()
    m1 = cp(11, left, mate)
    l0[1].wait_recv()
    m2 = cp(12, right, mate)
    z0[1].wait_recv()
    zl.append(cp(13, zp, left, hi))
    zr.append(cp(14, zp, right, hi))
    m3 = cp(15, zp, mate)
    h0 = hp(0, tme, tzp)
    scores(left)
    f1.wait_recv()
    m4 = cp(16, opp, mate, lo)
    f2.wait_recv()
    m5 = cp(17, opp, mate, hi)
    scores(right)
    scores(opp)
    m1.wait_recv()
    scores(at(zh, x + 3, 1 - core))
    zright, zleft, zopp = at(1 - zh, x + 1, core), at(1 - zh, x + 3, core), at(1 - zh, x + 2, core)
    zr[0].wait_recv()
    f3 = cp(18, zleft, right, lo)
    m2.wait_recv()
    scores(at(zh, x + 1, 1 - core))
    m4.wait_recv()
    m5.wait_recv()
    scores(at(zh, x + 2, 1 - core))
    raise_top(0)
    zl[1].wait_recv()
    f4 = cp(19, zright, left, hi)
    zr[1].wait_recv()
    m6 = cp(20, zleft, mate)
    zl[0].wait_recv()
    m7 = cp(21, zright, mate)
    near_low = jnp.maximum(first, zh * 8)
    near_mid = (near_low + me + 1) // 2
    weigh(near_low, near_mid, always, 0)
    f3.wait_recv()
    m8 = cp(22, zopp, mate, lo)
    f4.wait_recv()
    m9 = cp(23, zopp, mate, hi)
    weigh(near_mid, me + 1, always, 0)
    h0.wait_recv()
    h1.wait_recv()
    h2.wait_recv()
    h5 = hp(5, tdown, tup, pl.ds(0, 128))
    h6 = hp(6, tup, tdown, pl.ds(128, 128))
    h3 = hp(3, tzp, tup)
    h4 = hp(4, tzp, tdown)
    scores(zp)
    scores(zleft)
    scores(zright)
    m3.wait_recv()
    scores(at(1 - zh, x, 1 - core))
    m6.wait_recv()
    scores(at(1 - zh, x + 3, 1 - core))
    m7.wait_recv()
    scores(at(1 - zh, x + 1, 1 - core))
    raise_top(1)
    far = lax.rem(x + 2, 4)
    away = (1 - zh) * 8
    weigh(away, away + 8, lambda j: lax.rem(j // 2, 4) != far, 1)
    scores(zopp)
    m8.wait_recv()
    m9.wait_recv()
    scores(at(1 - zh, x + 2, 1 - core))
    raise_top(2)
    weigh(away + 2 * far, away + 2 * far + 2, always, 2)

    logs[...] = (
        kvall[:, rows, :groups].astype(F32)
        + kvall[:, rows + 1, :groups].astype(F32)
        + kvall[:, rows + 2, :groups].astype(F32)
    )
    for h in range(heads):
        inverse = 1.0 / local[size : size + 1, lanes_of(h)]
        out = local[:size, lanes_of(h)] * inverse
        corr = jnp.sum(out * g4[h].astype(F32).T, axis=0, keepdims=True)
        stat[h] = jnp.broadcast_to(corr, (8, rows))
        last = top[2, h]
        for group in range(3):
            top[group, h] = inverse * jnp.exp((top[group, h] - last) * scaling)

    h5.wait_recv()
    h7 = hp(7, topp, tzp, pl.ds(0, 128))
    h6.wait_recv()
    h8 = hp(8, topp, tzp, pl.ds(128, 128))

    def grads(d, c_at):
        def one_z(n, _):
            z = jnp.where(n == 0, 1 - zh, zh)
            group = jnp.where(n == 0, 2 if d == 2 else 1, 0)
            j = at(z, x + d, c_at)

            @pl.when((j <= me) & (j >= first))
            def _():
                k = kvall[j, :rows, :size]
                v = kvall[j, :rows, size:]
                for h in range(heads):
                    t = s_ref[j - first, h] * top[group, h, 0:1, :]
                    e = t * (dot(v, g4[h], (1, 1)) - stat[h, 0:1, :])
                    t4[:, lanes_of(h)] = t.astype(BF16)
                    d4[:, lanes_of(h)] = e.astype(BF16)
                y_acc[:size] += dot(k.astype(F32).T.astype(BF16), d4[...], (1, 0))
                dk = dot(d4[...], q4[...].reshape(heads * rows, size), (1, 0))
                dv = dot(t4[...], g4[...].reshape(heads * rows, size), (1, 0))
                p[z, lax.rem(x + d, 4), c_at] = jnp.concatenate([dk * scaling, dv], axis=1).astype(BF16)

            return 0

        lax.fori_loop(0, 2, one_z, 0)

    half = rows // 2
    low, high = pl.ds(0, half), pl.ds(half, half)

    def sp(k, src, dst, to):
        copy = remote(src, dst, ssem.at[24 + k], rsem.at[24 + k], (to, tp))
        copy.start()
        sent.append(copy)
        return copy

    def to_mate(k, d):
        grads(d, 1 - core)
        return sp(k, p.at[:, lax.rem(x + d, 4), 1 - core], got.at[d], mate)

    def both(d, z):
        return p[z, lax.rem(x + d, 4), core].astype(F32) + got[d, z].astype(F32)

    order = (1 - zh, zh)
    g2 = to_mate(0, 2)
    grads(2, core)
    g2.wait_recv()
    t0, t1, u0, u1 = [], [], [], []
    for n, z in enumerate(order):
        tout[z] = both(2, z).astype(BF16)
        t0.append(sp(4 + n, tout.at[z, low], uin.at[0, z], right))
        t1.append(sp(6 + n, tout.at[z, high], uin.at[1, z], left))
    g1 = to_mate(1, 1)
    grads(1, core)
    g3 = to_mate(2, 3)
    grads(3, core)
    g1.wait_recv()
    g3.wait_recv()
    for n, z in enumerate(order):
        u = both(1, z)
        uout[0, z, high] = u[half:].astype(BF16)
        t0[n].wait_recv()
        uout[0, z, low] = (u[:half] + uin[0, z].astype(F32)).astype(BF16)
        u0.append(sp(8 + n, uout.at[0, z], vin.at[0, z], right))
        u = both(3, z)
        uout[1, z, low] = u[:half].astype(BF16)
        t1[n].wait_recv()
        uout[1, z, high] = (u[half:] + uin[1, z].astype(F32)).astype(BF16)
        u1.append(sp(10 + n, uout.at[1, z], vin.at[1, z], left))
    g0 = to_mate(3, 0)
    grads(0, core)
    for h in range(heads):
        dq_ref[:, h * size : (h + 1) * size] = (y_acc[:size, lanes_of(h)].T * scaling).astype(BF16)
    g0.wait_recv()

    def whole(n, z):
        u0[n].wait_recv()
        u1[n].wait_recv()
        return (
            p[z, x, core].astype(F32)
            + got[0, z].astype(F32)
            + vin[0, z].astype(F32)
            + vin[1, z].astype(F32)
        )

    zout[...] = whole(0, 1 - zh).astype(BF16)
    zc = sp(12, zout, zin, zp)
    kept = whole(1, zh)
    zc.wait_recv()
    kvg_ref[...] = (kept + zin[...].astype(F32)).astype(BF16)
    h3.wait_recv()
    h4.wait_recv()
    h7.wait_recv()
    h8.wait_recv()
    for copy in sent:
        copy.wait_send()

    width = up_ref.shape[1]
    inner = mixed.shape[1]
    state_size = inner // groups

    def part(k):
        return pl.ds(pl.multiple_of(k * width, width), width)

    for index, value in enumerate(prefix_weights(logs[...], groups)):
        w_ref[index] = value
    weights[0].wait()
    weights[1].wait()
    for load in more:
        load.wait()

    def attn_term(k):
        return dot(dq_ref[...], qw[part(k)], (1, 1)) + dot(kvg_ref[...], kw[part(k)], (1, 1))

    spot = lax.broadcasted_iota(jnp.int32, (groups, inner), 1)
    head = lax.broadcasted_iota(jnp.int32, (groups, inner), 0) * state_size
    wide = jnp.where((spot >= head) & (spot < head + state_size), 1.0, 0.0).astype(BF16)

    def widen(value):
        high = value.astype(BF16)
        low = (value - high.astype(F32)).astype(BF16)
        return dot(high, wide, (1, 0)) + dot(low, wide, (1, 0))

    def mix():
        local[...] = widen(jnp.exp(cum_ref[...]))
        weights[3].wait()

        def step(k, _):
            y_acc[...] += dot(hid[k], mw[part(k)], (1, 0))
            return 0

        y_acc[...] = jnp.zeros_like(y_acc)
        lax.fori_loop(0, 8, step, 0)
        mixed[...] = y_acc[...].astype(BF16)

    mid = sent_sums(
        attn_term, lambda: up_ref[...].astype(F32), (tin, tuin, rin, rv, rout), 0, tssem, trsem, mix
    ).astype(BF16)
    mid_ref[...] = mid
    weights[2].wait()
    y_acc[...] = jnp.zeros_like(y_acc)

    def out_term(k):
        y_acc[...] += dot(everyone[k], ow[:, part(k)], (1, 1))

    spread_out(mid, everyone, 14, tssem, trsem, out_term)
    y[...] = y_acc[...].astype(BF16)

    cum = cum_ref[...]
    count = groups // 2
    begin = core * count
    half = count // 2
    theirs_at = pl.ds((1 - core) * count, count)
    ours = pl.ds(begin, count)
    copies = []

    def pp(k, src, dst, to):
        copy = remote(src, dst, tssem.at[28 + k], trsem.at[28 + k], (to, tp))
        copy.start()
        copies.append(copy)
        return copy

    wide_half = inner // 2

    def state_terms(c_at):
        lanes = pl.ds(pl.multiple_of(c_at * wide_half, wide_half), wide_half)
        weighted = (y[:, lanes].astype(F32) * local[:, lanes]).astype(BF16)
        found = dot(weighted, c_ref[...], (0, 0)).reshape((count,) + terms.shape[1:])
        terms[pl.ds(c_at * count, count)] = found
        ours_out[pl.ds(c_at * count, count)] = found.astype(BF16)

    state_terms(1 - core)
    a_heads, b_heads = pl.ds(0, half), pl.ds(half, half)
    away_at = (1 - core) * count
    c0 = [
        pp(n, ours_out.at[pl.ds(away_at + n * half, half)], theirs.at[pl.ds(away_at + n * half, half)], mate)
        for n in range(2)
    ]
    state_terms(core)
    c1 = pp(2, ours_out.at[ours], theirs.at[ours], mate)

    def w(k, h):
        return w_ref[k, pl.ds(begin + h, 1), :]

    inner_bc = dot(b_ref[...], c_ref[...], (1, 1))
    later = col >= row
    left_lane = lax.broadcasted_iota(jnp.int32, (rows, 2 * state_size), 1) < state_size

    def decay(h):
        spread = cumt_ref[pl.ds(h, 1), :] - cum_ref[:, h : h + 1]
        return jnp.exp(jnp.where(later, spread, -1e30))

    def pair_of(ref, p):
        both = ref[:, p * 2 * state_size : (p + 1) * 2 * state_size]
        none = jnp.zeros_like(both)
        return jnp.where(left_lane, both, none), jnp.where(left_lane, none, both), both

    def local_pairs(start, stop):
        for p in range(start, stop):
            y0, y1, _ = pair_of(y, p)
            a0 = (inner_bc * decay(2 * p)).astype(BF16)
            a1 = (inner_bc * decay(2 * p + 1)).astype(BF16)
            local[:, p * 2 * state_size : (p + 1) * 2 * state_size] = dot(a0, y0, (1, 0)) + dot(a1, y1, (1, 0))

    def chip_terms(n):
        c0[n].wait_recv()
        for h in range(n * half, (n + 1) * half):
            gx[0, h] = (
                w(0, h) * terms[begin + h] + w(1, h) * theirs[begin + h].astype(F32)
            ).astype(BF16)

    chip_terms(0)
    r0a = pp(3, gx.at[0, a_heads], gx.at[3, a_heads], right)
    chip_terms(1)
    l0b = pp(4, gx.at[0, b_heads], gx.at[1, b_heads], left)
    l0a = pp(5, gx.at[0, a_heads], gx.at[1, a_heads], left)
    r0b = pp(6, gx.at[0, b_heads], gx.at[3, b_heads], right)
    local_pairs(0, 2)
    r0a.wait_recv()
    r1 = pp(7, gx.at[3, a_heads], gx.at[2, a_heads], right)
    l0b.wait_recv()
    l1 = pp(8, gx.at[1, b_heads], gx.at[2, b_heads], left)
    local_pairs(2, 5)

    def weigh_states(base, h):
        return sum(w(base + d, h) * gx[d, h].astype(F32) for d in range(4))

    l0a.wait_recv()
    r1.wait_recv()
    for h in range(half):
        hout[h] = weigh_states(2, h).astype(BF16)
    z0a = pp(9, hout.at[a_heads], hin.at[a_heads], zp)
    r0b.wait_recv()
    l1.wait_recv()
    for h in range(half, count):
        hout[h] = weigh_states(2, h).astype(BF16)
    z0b = pp(10, hout.at[b_heads], hin.at[b_heads], zp)
    local_pairs(5, 8)
    stepping = widen(steps[...])
    y_acc[...] = stepping * widen(jnp.exp(cum_ref[pl.ds(rows - 1, 1)] - cum))
    local[...] = stepping * local[...] + widen(
        jnp.broadcast_to(skip_ref[...], (rows, groups))
    ) * y[...].astype(F32)
    e0 = []
    for n, (z_n, part_n) in enumerate(((z0a, a_heads), (z0b, b_heads))):
        z_n.wait_recv()
        for h in range(n * half, (n + 1) * half):
            eout[h] = (weigh_states(6, h) + w(10, h) * hin[h].astype(F32)).astype(BF16)
        e0.append(pp(11 + n, eout.at[part_n], ein.at[part_n], mate))
    c1.wait_recv()

    def finish(start, e):
        for h in range(count):
            at_h = pl.ds(start + h, 1)
            carried[start + h] = (
                w_ref[12, at_h, :] * theirs[start + h].astype(F32)
                + w_ref[11, at_h, :] * e[h].astype(F32)
            ).astype(BF16)

    finish(begin, eout)
    for copy in e0:
        copy.wait_recv()
    finish((1 - core) * count, ein)
    state = carried[...].reshape(inner, terms.shape[2])
    grad_in = (local[...] + dot(b_ref[...], state, (1, 1)) * y_acc[...]).astype(BF16)

    def mix_term(k):
        return dot(grad_in, mw[part(k)], (1, 1))

    def states():
        scaled = (mixed[...].astype(F32) * y_acc[...]).astype(BF16)
        s_ref[0, 0] = jnp.zeros((rows, rows), F32)
        for p in range(groups // 2):
            m0, m1, _ = pair_of(mixed, p)
            both = y[:, p * 2 * state_size : (p + 1) * 2 * state_size]
            for h, m in ((2 * p, m0), (2 * p + 1, m1)):
                s_ref[0, 0] += dot(m, both, (1, 1)) * decay(h) * steps[:, h : h + 1]
        state_ref[...] = dot(s_ref[0, 0].astype(BF16), c_ref[...], (1, 0)) + dot(
            scaled, state, (1, 0)
        )

    hidden_ref[...] = sent_sums(
        mix_term, lambda: mid_ref[...].astype(F32), (tin, tuin, rin, rv, rout), 42, tssem, trsem, states
    ).astype(BF16)
    for copy in copies:
        copy.wait_send()


def whole(arrays, cid):
    keyval, query, _, hidden, qw, kw, ow, mw, upstream, b, c, step = arrays[:12]
    rows, cols = keyval.shape
    size = cols // 2
    heads = query.shape[1] // size
    groups = step.shape[0]
    inner = mw.shape[1]
    full = upstream.shape
    state = (groups, inner // groups, b.shape[1])
    part = (groups // 2,) + state[1:]
    any_spec = pl.BlockSpec(memory_space=pl.ANY)
    two = (2, rows, cols)
    vm = pltpu.VMEM
    dma = pltpu.SemaphoreType.DMA
    return pl.pallas_call(
        whole_kernel,
        out_shape=(
            jax.ShapeDtypeStruct(full, BF16),
            jax.ShapeDtypeStruct(full, BF16),
            jax.ShapeDtypeStruct((rows, b.shape[1]), F32),
        ),
        in_specs=[any_spec] * 11 + [VM] * 4,
        out_specs=(VM,) * 3,
        scratch_shapes=[
            vm((rows + 16, cols), BF16),
            vm((16, rows + 16, cols), BF16),
            vm((13, heads, rows, rows), F32),
            vm((heads, rows, size), BF16),
            vm((heads, rows, size), BF16),
            vm((heads, 8, rows), F32),
            vm((3, heads, 8, rows), F32),
            vm((rows, heads * rows), BF16),
            vm((rows, heads * rows), BF16),
            vm((2, 4, 2, rows, cols), BF16),
            vm((4,) + two, BF16),
            vm((2, 2, rows // 2, cols), BF16),
            vm((2,) + two, BF16),
            vm((rows, cols), BF16),
            vm(two, BF16),
            vm((2,) + two, BF16),
            vm((rows, cols), BF16),
            vm(query.shape, BF16),
            vm(keyval.shape, BF16),
            vm((8,) + hidden.shape, BF16),
            vm((rows, groups), F32),
            vm((groups, rows), F32),
            vm((rows, groups), F32),
            vm((16, groups), F32),
            vm(qw.shape, BF16),
            vm(kw.shape, BF16),
            vm(ow.shape, BF16),
            vm(mw.shape, BF16),
            vm(full, BF16),
            vm(b.shape, BF16),
            vm(c.shape, BF16),
            vm(full, BF16),
            vm((2, rows // 2, full[1]), BF16),
            vm((4,) + full, BF16),
            vm(full, BF16),
            vm((7,) + full, BF16),
            vm((8,) + full, BF16),
            vm((rows, inner), F32),
            vm((rows, inner), BF16),
            vm((rows, inner), BF16),
            vm((rows, inner), F32),
            vm((13, groups, 128), F32),
            vm(state, F32),
            vm(state, BF16),
            vm(state, BF16),
            vm((4,) + part, BF16),
            vm(part, BF16),
            vm(part, BF16),
            vm(part, BF16),
            vm(part, BF16),
            vm(state, BF16),
            dma((37,)),
            dma((37,)),
            dma((9,)),
            dma((9,)),
            dma((56,)),
            dma((56,)),
            dma((17,)),
        ],
        compiler_params=pltpu.CompilerParams(
            collective_id=cid, has_side_effects=True, vmem_limit_bytes=(64 << 20) - (256 << 10)
        ),
        name="whole",
    )(*arrays)


def finish_kernel(a_ref, b_ref, c_ref, a_out, b_out, c_out):
    a_out[...] = a_ref[...]
    b_out[...] = b_ref[...]
    c_out[...] = c_ref[...]


def finish(arrays):
    return pl.pallas_call(
        finish_kernel,
        out_shape=tuple(jax.ShapeDtypeStruct(a.shape, a.dtype) for a in arrays),
        in_specs=[VM] * 3,
        out_specs=(VM,) * 3,
        name="finish",
    )(*arrays)


def on_device(
    hidden_in,
    upstream,
    query_ckpt,
    keyval_ckpt,
    attn_out_grad,
    segments,
    query_weight,
    keyval_weight,
    mix_weight,
    out_weight,
    state_in_ckpt,
    state_out_ckpt,
    step_size,
    decay_rate,
    skip_gain,
):
    return finish(
        whole(
            (
                keyval_ckpt,
                query_ckpt,
                attn_out_grad,
                hidden_in,
                query_weight,
                keyval_weight,
                out_weight,
                mix_weight,
                upstream,
                state_in_ckpt,
                state_out_ckpt,
                step_size.T,
                decay_rate[None, :],
                segments.reshape(-1, 128),
                skip_gain[None, :],
            ),
            1,
        )
    )


def solution(mesh):
    placed = (
        P("ctx", "tp"),
        P("ctx", "tp"),
        P("ctx", "tp"),
        P("ctx", "tp"),
        P("ctx", "tp"),
        P(),
        P(None, "tp"),
        P(None, "tp"),
        P(None, "tp"),
        P("tp", None),
        P("ctx", "tp"),
        P("ctx", "tp"),
        P("ctx", "tp"),
        P("tp"),
        P("tp"),
    )
    return jax.shard_map(
        on_device,
        mesh=mesh,
        in_specs=placed,
        out_specs=(P("ctx", "tp"), P("ctx", "tp"), P("ctx", "tp")),
        check_vma=False,
    )
```
